32 devices in a mesh: ctx: 8 (over z, x), tp: 4 (over y, core).
Axes of the slice: x: 2, y: 2, z: 4, core: 2. Of those that a mesh axis runs over, the one named last changes fastest.
Arguments:
- attn_query: bfloat16 [2048, 4096], P('ctx', 'tp'), may hold values from -8 to 8
- attn_key: bfloat16 [2048, 4096], P('ctx', 'tp'), may hold values from -8 to 8
- attn_value: bfloat16 [2048, 4096], P('ctx', 'tp'), may hold values from -6 to 6
- out_weight: bfloat16 [4096, 8192], P('tp'), may hold values from -0.125 to 0.125
Outputs:
- attn_out: bfloat16 [2048, 8192], P('ctx', 'tp')
The draws below stay inside these ranges and needn't reach their ends.
All inputs are finite; a program needn't handle non-finite values.
Results may differ from the reference program's by a relative error of at most 0.015.
Values may be sent and summed in bfloat16 or wider, within the bound.
No kernel may reach another device: no remote copies, remote signals or barrier semaphores. Data moves between devices by JAX's collectives and lax.ppermute only.
A program may use at most 128 MiB of HBM per device.

```python
import jax
import jax.numpy as jnp
from jax import lax

D = 8192
HEADS = 32
HD = 128
SEQ = 2048
N_TP = 4


def draw_attn_query(key, part):
    width = HEADS * HD
    base = jnp.clip(jax.random.normal(jax.random.fold_in(key, 1), (SEQ, width), jnp.float32), -8.0, 8.0)
    return base.astype(jnp.bfloat16)


def draw_attn_key(key, part):
    width = HEADS * HD
    base = jnp.clip(jax.random.normal(jax.random.fold_in(key, 2), (SEQ, width), jnp.float32), -8.0, 8.0)
    return base.astype(jnp.bfloat16)


def strengthened(values, key, source, target, blocks, factor):
    owner, partner = [(jnp.arange(values.shape[axis_at]) // (values.shape[axis_at] // blocks)).reshape([-1 if axis == axis_at else 1 for axis in range(values.ndim)]) for axis_at in (source, target)]
    chosen = jax.random.permutation(key, blocks)[partner]
    strong = (owner == chosen) | (owner == (partner + blocks // 2) % blocks)
    return jnp.where(strong, factor * values, values)


def block_levels(own_key, dims, pieces, low, top_value):
    level, own = 1.0, jax.random.fold_in(own_key, 6)
    for axis_at, blocks in pieces:
        steps = jnp.exp(jax.random.uniform(jax.random.fold_in(own, axis_at), (blocks,), jnp.float32, low / len(pieces), top_value / len(pieces)))
        level = level * jnp.repeat(steps, dims[axis_at] // blocks).reshape([-1 if axis == axis_at else 1 for axis in range(len(dims))])
    return level


def centred(stream_key, shape, scale, most, shards=(), held_as=jnp.bfloat16):
    array = scale * jax.random.normal(stream_key, shape, jnp.float32)
    if shards:
        array = array * block_levels(stream_key, shape, shards, -0.22, 0.18)
    return jnp.clip(array, -most, most).astype(held_as)


def bell_draw_with(own_key, extent, scale, bound, cuts, heavy, kind=jnp.bfloat16):
    array = scale * jax.random.normal(own_key, extent, jnp.float32)
    if cuts:
        array = array * block_levels(own_key, extent, cuts, -0.22, 0.18)
    return jnp.clip(strengthened(array, jax.random.fold_in(own_key, 3), *heavy), -bound, bound).astype(kind)


def setup_inputs(seed: int = 0) -> dict:
    arg_keys = jax.random.split(jax.random.key(seed), 5)
    return {
        "attn_query": draw_attn_query(jax.random.fold_in(arg_keys[4], 71), 0),
        "attn_key": draw_attn_key(jax.random.fold_in(arg_keys[4], 71), 0),
        "attn_value": centred(arg_keys[2], (SEQ, HEADS * HD), 1.0, 6.0, ((0, 8), (1, 4))),
        "out_weight": bell_draw_with(arg_keys[3], (HEADS * HD, D), (HEADS * HD) ** -0.5, 0.125, ((0, 4),), (0, 1, 4, 2.0)),
    }


def reference(attn_query, attn_key, attn_value, out_weight):
    scale = HD ** -0.5
    span_rows = 512 if SEQ % 512 == 0 else SEQ
    queries = attn_query.reshape(SEQ, HEADS, HD).astype(jnp.float32)
    keys = attn_key.reshape(SEQ, HEADS, HD).astype(jnp.float32)
    values = attn_value.reshape(SEQ, HEADS, HD).astype(jnp.float32)
    key_pos = jnp.arange(SEQ, dtype=jnp.int32)

    def one_block(start):
        block = lax.dynamic_slice_in_dim(queries, start, span_rows, 0)
        query_pos = start + jnp.arange(span_rows, dtype=jnp.int32)
        scores = jnp.einsum("qhd,khd->hqk", block, keys) * scale
        allowed = key_pos[None, None, :] <= query_pos[None, :, None]
        largest = jnp.max(jnp.where(allowed, scores, -1e30), axis=-1)
        weights = jnp.where(allowed, jnp.exp(scores - largest[..., None]), 0.0)
        totals = jnp.sum(weights, axis=-1)
        probs = weights.astype(jnp.bfloat16).astype(jnp.float32)
        numer = jnp.einsum("hqk,khd->qhd", probs, values)
        return (numer / jnp.transpose(totals)[..., None]).astype(jnp.bfloat16)

    starts = jnp.arange(SEQ // span_rows, dtype=jnp.int32) * span_rows
    heads = lax.map(one_block, starts).reshape(SEQ, HEADS * HD)

    group = HEADS * HD // N_TP

    def add_group(index, total):
        cols = lax.dynamic_slice_in_dim(heads, index * group, group, 1)
        rows = lax.dynamic_slice_in_dim(out_weight, index * group, group, 0)
        partial_value = jnp.dot(cols, rows, preferred_element_type=jnp.float32).astype(jnp.bfloat16)
        partial_value = lax.optimization_barrier(partial_value)
        return total + partial_value.astype(jnp.float32)

    summed = lax.fori_loop(0, N_TP, add_group, jnp.zeros((SEQ, D), jnp.float32))
    return summed.astype(jnp.bfloat16)
```

```python
import functools

import jax
import jax.numpy as jnp
from jax import lax
from jax.experimental import pallas as pl
from jax.experimental.pallas import tpu as pltpu
from jax.sharding import PartitionSpec as P

HD = 128
MIB = 1 << 20
VMEM = pl.BlockSpec(memory_space=pltpu.VMEM)


def params(mib):
    return pltpu.CompilerParams(vmem_limit_bytes=mib * MIB)


def attend(queries, keys, values, query_pos):
    rows = queries.shape[0]
    local_heads = queries.shape[1] // HD
    scale = HD ** (-0.5)
    shaped_q = queries.reshape(rows, local_heads, HD)
    latest = jnp.max(query_pos)
    initial = (
        jnp.full((local_heads, rows), -1e30, jnp.float32),
        jnp.zeros((local_heads, rows), jnp.float32),
        jnp.zeros((local_heads, rows, HD), jnp.float32),
    )
    piece_keys = lax.all_gather(keys, "ctx", axis=0, tiled=True)
    piece_values = lax.all_gather(values, "ctx", axis=0, tiled=True)
    count_rows = piece_keys.shape[0]
    span_rows = 2 * rows

    def one_block(block, state):
        offset = block * span_rows
        block_keys = lax.dynamic_slice_in_dim(piece_keys, offset, span_rows, 0).reshape(
            span_rows, local_heads, HD
        )
        block_values = lax.dynamic_slice_in_dim(piece_values, offset, span_rows, 0).reshape(
            span_rows, local_heads, HD
        )
        key_pos = offset + jnp.arange(span_rows, dtype=jnp.int32)

        def compute(inner):
            maxes, totals, accum = inner
            scores = (
                jnp.einsum("qhd,khd->hqk", shaped_q, block_keys, preferred_element_type=jnp.float32)
                * scale
            )
            allowed = key_pos[None, None, :] <= query_pos[None, :, None]
            new_max = jnp.maximum(maxes, jnp.max(jnp.where(allowed, scores, -1e30), axis=-1))
            factor = jnp.exp(maxes - new_max)
            weights = jnp.where(allowed, jnp.exp(scores - new_max[..., None]), 0.0)
            totals = totals * factor + jnp.sum(weights, axis=-1)
            accum = accum * factor[..., None] + jnp.einsum(
                "hqk,khd->hqd",
                weights.astype(jnp.bfloat16),
                block_values,
                preferred_element_type=jnp.float32,
            )
            return (new_max, totals, accum)

        return lax.cond(jnp.min(key_pos) <= latest, compute, lambda inner: inner, state)

    maxes, totals, accum = lax.fori_loop(0, count_rows // span_rows, one_block, initial)
    result = accum / totals[..., None]
    return jnp.transpose(result, (1, 0, 2)).reshape(rows, local_heads * HD).astype(jnp.bfloat16)


def gather_form(attn_query, attn_key, attn_value, out_weight):
    rows = attn_query.shape[0]
    query_pos = lax.axis_index("ctx") * rows + jnp.arange(rows, dtype=jnp.int32)
    heads = attend(attn_query, attn_key, attn_value, query_pos)
    partial_value = jnp.dot(heads, out_weight, preferred_element_type=jnp.float32)
    return lax.psum_scatter(
        partial_value.astype(jnp.bfloat16), "tp", scatter_dimension=1, tiled=True
    )


def pack_kernel(n, me_ref, q_ref, k_ref, v_ref, *outs):
    rows = q_ref.shape[0]
    for shift in range(n):
        head = lax.rem(me_ref[0] + shift, n)
        cols = pl.ds(pl.multiple_of(head * HD, HD), HD)
        for part, ref in enumerate((q_ref, k_ref, v_ref)):
            outs[shift][part * rows : (part + 1) * rows, :] = ref[:, cols]


def attention_kernel(n, me_ref, *refs):
    packed, outs = refs[:n], refs[n : 2 * n]
    q_all, k_all, v_all, o_all = refs[2 * n :]
    rows = packed[0].shape[0] // 3
    me = me_ref[0]
    for shift in range(n):
        block = lax.rem(me - shift + n, n)
        at = pl.ds(pl.multiple_of(block * rows, rows), rows)
        q_all[at, :] = packed[shift][0:rows, :]
        k_all[at, :] = packed[shift][rows : 2 * rows, :]
        v_all[at, :] = packed[shift][2 * rows : 3 * rows, :]
    factor = HD ** (-0.5) * 1.4426950408889634
    diag = lax.broadcasted_iota(jnp.int32, (rows, rows), 1) <= lax.broadcasted_iota(
        jnp.int32, (rows, rows), 0
    )
    for block in range(n):
        lo, hi = block * rows, (block + 1) * rows
        query = q_all[lo:hi, :]
        dims = (((1,), (1,)), ((), ()))
        last = lax.dot_general(query, k_all[lo:hi, :], dims, preferred_element_type=jnp.float32)
        last = jnp.where(diag, last, -1e30)
        top = jnp.max(last, axis=1, keepdims=True)
        if block:
            early = lax.dot_general(
                query, k_all[0:lo, :], dims, preferred_element_type=jnp.float32
            )
            top = jnp.maximum(top, jnp.max(early, axis=1, keepdims=True))
        w_last = jnp.where(diag, jnp.exp2((last - top) * factor), 0.0)
        total = jnp.sum(w_last, axis=1, keepdims=True)
        acc = jnp.dot(
            w_last.astype(jnp.bfloat16), v_all[lo:hi, :], preferred_element_type=jnp.float32
        )
        if block:
            w_early = jnp.exp2((early - top) * factor)
            total += jnp.sum(w_early, axis=1, keepdims=True)
            acc += jnp.dot(
                w_early.astype(jnp.bfloat16), v_all[0:lo, :], preferred_element_type=jnp.float32
            )
        o_all[lo:hi, :] = (acc / total).astype(jnp.bfloat16)
    for shift in range(n):
        block = lax.rem(me + shift, n)
        outs[shift][...] = o_all[pl.ds(pl.multiple_of(block * rows, rows), rows), :]


def project_kernel(n, tiles, scalar_ref, *refs):
    pieces, w_ref, outs, heads = refs[:n], refs[n], refs[n + 1 : n + 3], refs[n + 3]
    step = pl.program_id(0)

    @pl.when(step == 0)
    def _():
        for shift in range(n):
            head = lax.rem(scalar_ref[0] - shift + n, n)
            heads[:, pl.ds(pl.multiple_of(head * HD, HD), HD)] = pieces[shift][...]

    product = jnp.dot(heads[...], w_ref[...], preferred_element_type=jnp.float32)
    for which in range(2):

        @pl.when(step // tiles == which)
        def _():
            outs[which][...] = product.astype(jnp.bfloat16)


def project(scalars, pieces, weight, cols, tile):
    n, rows = len(pieces), pieces[0].shape[0]
    depth = weight.shape[0]
    tiles = cols // tile
    out = jax.ShapeDtypeStruct((rows, cols), jnp.bfloat16)
    return pl.pallas_call(
        functools.partial(project_kernel, n, tiles),
        grid_spec=pltpu.PrefetchScalarGridSpec(
            num_scalar_prefetch=1,
            grid=(2 * tiles,),
            in_specs=[pl.BlockSpec((rows, HD), lambda i, s: (0, 0)) for _ in range(n)]
            + [
                pl.BlockSpec(
                    (depth, tile),
                    lambda i, s: (0, jnp.where(i < tiles, s[1], s[2]) * tiles + lax.rem(i, tiles)),
                )
            ],
            out_specs=[
                pl.BlockSpec((rows, tile), lambda i, s: (0, jnp.minimum(i, tiles - 1))),
                pl.BlockSpec((rows, tile), lambda i, s: (0, jnp.maximum(i - tiles, 0))),
            ],
            scratch_shapes=[pltpu.VMEM((rows, depth), jnp.bfloat16)],
        ),
        out_shape=[out, out],
        compiler_params=params(40),
        cost_estimate=pl.CostEstimate(
            flops=4 * rows * depth * cols, bytes_accessed=4 * depth * cols, transcendentals=0
        ),
    )(scalars, *pieces, weight)


def heads_form(attn_query, attn_key, attn_value, out_weight):
    n = lax.axis_size("ctx")
    tp = lax.axis_size("tp")
    rows = attn_query.shape[0]
    me = lax.axis_index("ctx")
    mine = lax.axis_index("tp")
    me_arr = me.astype(jnp.int32).reshape(1)
    smem = pl.BlockSpec(memory_space=pltpu.SMEM)
    order = sorted(range(1, n), key=lambda s: -min(s, n - s))

    def around(arrays):
        got = [arrays[0]] + [None] * (n - 1)
        for shift in order:
            got[shift] = lax.ppermute(
                arrays[shift], "ctx", [(i, (i + shift) % n) for i in range(n)]
            )
        return got

    packed = pl.pallas_call(
        functools.partial(pack_kernel, n),
        in_specs=[smem] + [VMEM] * 3,
        out_specs=[VMEM] * n,
        out_shape=[jax.ShapeDtypeStruct((3 * rows, HD), jnp.bfloat16)] * n,
        compiler_params=params(16),
    )(me_arr, attn_query, attn_key, attn_value)
    packed = around(packed)
    pairs = n * (n + 1) // 2
    outs = pl.pallas_call(
        functools.partial(attention_kernel, n),
        in_specs=[smem] + [VMEM] * n,
        out_specs=[VMEM] * n,
        out_shape=[jax.ShapeDtypeStruct((rows, HD), jnp.bfloat16)] * n,
        scratch_shapes=[pltpu.VMEM((n * rows, HD), jnp.bfloat16)] * 4,
        compiler_params=params(40),
        cost_estimate=pl.CostEstimate(
            flops=4 * pairs * rows * rows * HD,
            bytes_accessed=8 * n * rows * HD,
            transcendentals=pairs * rows * rows,
        ),
    )(me_arr, *packed)
    pieces = around(outs)

    cols = out_weight.shape[1] // tp
    half = tp // 2
    y, core = mine // 2, lax.rem(mine, 2)
    swap = [(i, i ^ 1) for i in range(tp)]

    def wanted(plane):
        return jnp.stack([me, 2 * plane + 1 - core, 2 * plane + core]).astype(jnp.int32)

    f32 = jnp.float32
    crossing = []
    for shift in range(1, half):
        plane = lax.rem(y + shift, half)
        give, keep = project(wanted(plane), pieces, out_weight, cols, 512)
        both = (keep.astype(f32) + lax.ppermute(give, "tp", swap).astype(f32)).astype(jnp.bfloat16)
        crossing.append(
            lax.ppermute(both, "tp", [(i, (i + 2 * shift) % tp) for i in range(tp)])
        )
    give, keep = project(wanted(y), pieces, out_weight, cols, 512)
    total = keep.astype(f32) + lax.ppermute(give, "tp", swap).astype(f32)
    for one in crossing:
        total += one.astype(f32)
    return total.astype(jnp.bfloat16)


def solution(mesh):
    def per_device(attn_query, attn_key, attn_value, out_weight):
        heads = attn_query.shape[1] // HD
        form = heads_form if heads == mesh.shape["ctx"] else gather_form
        return form(attn_query, attn_key, attn_value, out_weight)

    return jax.shard_map(
        per_device,
        mesh=mesh,
        in_specs=(P("ctx", "tp"), P("ctx", "tp"), P("ctx", "tp"), P("tp", None)),
        out_specs=P("ctx", "tp"),
        check_vma=False,
    )
```

```python
import functools

import jax
import jax.numpy as jnp
from jax import lax
from jax.experimental import pallas as pl
from jax.experimental.pallas import tpu as pltpu
from jax.sharding import PartitionSpec as P

HD = 128
MIB = 1 << 20
OWN_PARTS = 2
FETCH_MIB = 40
COST = pl.CostEstimate(flops=1, bytes_accessed=1, transcendentals=1)
VMEM = pl.BlockSpec(memory_space=pltpu.VMEM)


def params(mib):
    return pltpu.CompilerParams(vmem_limit_bytes=mib * MIB)


def attend(queries, keys, values, query_pos):
    rows = queries.shape[0]
    local_heads = queries.shape[1] // HD
    scale = HD ** (-0.5)
    shaped_q = queries.reshape(rows, local_heads, HD)
    latest = jnp.max(query_pos)
    initial = (
        jnp.full((local_heads, rows), -1e30, jnp.float32),
        jnp.zeros((local_heads, rows), jnp.float32),
        jnp.zeros((local_heads, rows, HD), jnp.float32),
    )
    piece_keys = lax.all_gather(keys, "ctx", axis=0, tiled=True)
    piece_values = lax.all_gather(values, "ctx", axis=0, tiled=True)
    count_rows = piece_keys.shape[0]
    span_rows = 2 * rows

    def one_block(block, state):
        offset = block * span_rows
        block_keys = lax.dynamic_slice_in_dim(piece_keys, offset, span_rows, 0).reshape(
            span_rows, local_heads, HD
        )
        block_values = lax.dynamic_slice_in_dim(piece_values, offset, span_rows, 0).reshape(
            span_rows, local_heads, HD
        )
        key_pos = offset + jnp.arange(span_rows, dtype=jnp.int32)

        def compute(inner):
            maxes, totals, accum = inner
            scores = (
                jnp.einsum("qhd,khd->hqk", shaped_q, block_keys, preferred_element_type=jnp.float32)
                * scale
            )
            allowed = key_pos[None, None, :] <= query_pos[None, :, None]
            new_max = jnp.maximum(maxes, jnp.max(jnp.where(allowed, scores, -1e30), axis=-1))
            factor = jnp.exp(maxes - new_max)
            weights = jnp.where(allowed, jnp.exp(scores - new_max[..., None]), 0.0)
            totals = totals * factor + jnp.sum(weights, axis=-1)
            accum = accum * factor[..., None] + jnp.einsum(
                "hqk,khd->hqd",
                weights.astype(jnp.bfloat16),
                block_values,
                preferred_element_type=jnp.float32,
            )
            return (new_max, totals, accum)

        return lax.cond(jnp.min(key_pos) <= latest, compute, lambda inner: inner, state)

    maxes, totals, accum = lax.fori_loop(0, count_rows // span_rows, one_block, initial)
    result = accum / totals[..., None]
    return jnp.transpose(result, (1, 0, 2)).reshape(rows, local_heads * HD).astype(jnp.bfloat16)


def gather_form(attn_query, attn_key, attn_value, out_weight):
    rows = attn_query.shape[0]
    query_pos = lax.axis_index("ctx") * rows + jnp.arange(rows, dtype=jnp.int32)
    heads = attend(attn_query, attn_key, attn_value, query_pos)
    partial_value = jnp.dot(heads, out_weight, preferred_element_type=jnp.float32)
    return lax.psum_scatter(
        partial_value.astype(jnp.bfloat16), "tp", scatter_dimension=1, tiled=True
    )


def pack_kernel(n, me_ref, q_ref, k_ref, v_ref, *refs):
    outs, (held, sem) = refs[:n], refs[n:]
    rows = q_ref.shape[0]
    copies = [
        pltpu.make_async_copy(ref, held.at[part], sem.at[part])
        for part, ref in enumerate((q_ref, k_ref, v_ref))
    ]
    for one in copies:
        one.start()
    for part, one in enumerate(copies):
        one.wait()
        for shift in range(n):
            head = lax.rem(me_ref[0] + shift, n)
            cols = pl.ds(pl.multiple_of(head * HD, HD), HD)
            outs[shift][part * rows : (part + 1) * rows, :] = held[part, :, cols]


def attention_kernel(n, me_ref, *refs):
    packed, outs = refs[:n], refs[n : 2 * n]
    q_all, k_all, v_all, o_all = refs[2 * n :]
    rows = packed[0].shape[0] // 3
    me = me_ref[0]
    for shift in range(n):
        block = lax.rem(me - shift + n, n)
        at = pl.ds(pl.multiple_of(block * rows, rows), rows)
        q_all[at, :] = packed[shift][0:rows, :]
        k_all[at, :] = packed[shift][rows : 2 * rows, :]
        v_all[at, :] = packed[shift][2 * rows : 3 * rows, :]
    factor = HD ** (-0.5) * 1.4426950408889634
    diag = lax.broadcasted_iota(jnp.int32, (rows, rows), 1) <= lax.broadcasted_iota(
        jnp.int32, (rows, rows), 0
    )
    for block in range(n):
        lo, hi = block * rows, (block + 1) * rows
        query = q_all[lo:hi, :]
        dims = (((1,), (1,)), ((), ()))
        last = lax.dot_general(query, k_all[lo:hi, :], dims, preferred_element_type=jnp.float32)
        last = jnp.where(diag, last, -1e30)
        top = jnp.max(last, axis=1, keepdims=True)
        if block:
            early = lax.dot_general(
                query, k_all[0:lo, :], dims, preferred_element_type=jnp.float32
            )
            top = jnp.maximum(top, jnp.max(early, axis=1, keepdims=True))
        w_last = jnp.exp2((last - top) * factor)
        total = jnp.sum(w_last, axis=1, keepdims=True)
        acc = jnp.dot(
            w_last.astype(jnp.bfloat16), v_all[lo:hi, :], preferred_element_type=jnp.float32
        )
        if block:
            w_early = jnp.exp2((early - top) * factor)
            total += jnp.sum(w_early, axis=1, keepdims=True)
            acc += jnp.dot(
                w_early.astype(jnp.bfloat16), v_all[0:lo, :], preferred_element_type=jnp.float32
            )
        o_all[lo:hi, :] = (acc / total).astype(jnp.bfloat16)
    for shift in range(n):
        block = lax.rem(me + shift, n)
        outs[shift][...] = o_all[pl.ds(pl.multiple_of(block * rows, rows), rows), :]


def fetch_kernel(place_ref, w_ref, *refs):
    outs, sem = refs[:-1], refs[-1]
    cols = outs[0].shape[1]
    copies = []
    for which, out in enumerate(outs):
        at = pl.ds(pl.multiple_of(place_ref[1 + which], cols), cols)
        copies.append(pltpu.make_async_copy(w_ref.at[:, at], out, sem.at[which]))
    for one in copies:
        one.start()
    for one in copies:
        one.wait()


def fetch(place, weight, cols):
    depth, groups = weight.shape[0], place.shape[0] - 1
    return pl.pallas_call(
        fetch_kernel,
        in_specs=[pl.BlockSpec(memory_space=pltpu.SMEM), pl.BlockSpec(memory_space=pl.ANY)],
        out_specs=[VMEM] * groups,
        out_shape=[jax.ShapeDtypeStruct((depth, cols), weight.dtype)] * groups,
        scratch_shapes=[pltpu.SemaphoreType.DMA((groups,))],
        compiler_params=params(FETCH_MIB),
        cost_estimate=pl.CostEstimate(
            flops=1, bytes_accessed=4 * depth * cols * groups, transcendentals=1
        ),
    )(place, weight)


def project_kernel(n, tile, place_ref, *refs):
    pieces, (heads,) = refs[:n], refs[-1:]
    groups = (len(refs) - 1 - n) // 2
    weights, outs = refs[n : n + groups], refs[n + groups : -1]
    for shift in range(n):
        head = lax.rem(place_ref[0] - shift + n, n)
        heads[:, pl.ds(pl.multiple_of(head * HD, HD), HD)] = pieces[shift][...]
    for weight, out in zip(weights, outs):
        for at in range(0, out.shape[1], tile):
            out[:, at : at + tile] = jnp.dot(
                heads[...], weight[:, at : at + tile], preferred_element_type=jnp.float32
            ).astype(jnp.bfloat16)


def project(place, pieces, weights):
    n, rows = len(pieces), pieces[0].shape[0]
    depth, cols = weights[0].shape
    return pl.pallas_call(
        functools.partial(project_kernel, n, 512),
        in_specs=[pl.BlockSpec(memory_space=pltpu.SMEM)] + [VMEM] * (n + len(weights)),
        out_specs=[VMEM] * len(weights),
        out_shape=[jax.ShapeDtypeStruct((rows, cols), jnp.bfloat16)] * len(weights),
        scratch_shapes=[pltpu.VMEM((rows, depth), jnp.bfloat16)],
        compiler_params=params(16),
        cost_estimate=COST,
    )(place, *pieces, *weights)


def heads_form(attn_query, attn_key, attn_value, out_weight):
    n = lax.axis_size("ctx")
    tp = lax.axis_size("tp")
    rows = attn_query.shape[0]
    me = lax.axis_index("ctx")
    mine = lax.axis_index("tp")
    me_arr = me.astype(jnp.int32).reshape(1)
    smem = pl.BlockSpec(memory_space=pltpu.SMEM)
    order = sorted(range(1, n), key=lambda s: -min(s, n - s))

    def around(arrays):
        got = [arrays[0]] + [None] * (n - 1)
        for shift in order:
            got[shift] = lax.ppermute(
                arrays[shift], "ctx", [(i, (i + shift) % n) for i in range(n)]
            )
        return got

    packed = list(pl.pallas_call(
        functools.partial(pack_kernel, n),
        in_specs=[smem] + [pl.BlockSpec(memory_space=pl.ANY)] * 3,
        out_specs=[VMEM] * n,
        out_shape=[jax.ShapeDtypeStruct((3 * rows, HD), jnp.bfloat16)] * n,
        scratch_shapes=[
            pltpu.VMEM((3, rows, n * HD), jnp.bfloat16),
            pltpu.SemaphoreType.DMA((3,)),
        ],
        compiler_params=params(56),
        cost_estimate=COST,
    )(me_arr, attn_query, attn_key, attn_value))
    cols = out_weight.shape[1] // tp
    half = tp // 2
    y, core = mine // 2, lax.rem(mine, 2)
    swap = [(i, i ^ 1) for i in range(tp)]
    f32, bf16 = jnp.float32, jnp.bfloat16

    def wanted(plane):
        groups = [2 * plane + 1 - core, 2 * plane + core]
        return jnp.stack([me] + [group * cols for group in groups]).astype(jnp.int32)

    near = [fetch(wanted(lax.rem(y + shift, half)), out_weight, cols) for shift in range(1, half)]
    last = order[-1]
    packed[last], near = lax.optimization_barrier((packed[last], near))
    packed = around(packed)
    pairs = n * (n + 1) // 2
    outs = pl.pallas_call(
        functools.partial(attention_kernel, n),
        in_specs=[smem] + [VMEM] * n,
        out_specs=[VMEM] * n,
        out_shape=[jax.ShapeDtypeStruct((rows, HD), jnp.bfloat16)] * n,
        scratch_shapes=[pltpu.VMEM((n * rows, HD), jnp.bfloat16)] * 4,
        compiler_params=params(24),
        cost_estimate=pl.CostEstimate(
            flops=4 * pairs * rows * rows * HD,
            bytes_accessed=8 * n * rows * HD,
            transcendentals=pairs * rows * rows,
        ),
    )(me_arr, *packed)
    pieces = around(outs)

    crossing = []
    for shift, weights in enumerate(near, 1):
        plane = lax.rem(y + shift, half)
        perm = [(i, (i + 2 * shift) % tp) for i in range(tp)]
        give, keep = project(wanted(plane), pieces, weights)
        both = (keep.astype(f32) + lax.ppermute(give, "tp", swap).astype(f32)).astype(bf16)
        crossing.append(lax.ppermute(both, "tp", perm))
        both, *pieces = lax.optimization_barrier((both, *pieces))
    out_weight, *pieces = lax.optimization_barrier((out_weight, *pieces))
    give, keep = project(wanted(y), pieces, fetch(wanted(y), out_weight, cols))
    piece = cols // OWN_PARTS
    swapped = [
        lax.ppermute(give[:, at : at + piece], "tp", swap) for at in range(0, cols, piece)
    ]
    total = keep.astype(f32) + jnp.concatenate(swapped, axis=1).astype(f32)
    for one in crossing:
        total += one.astype(f32)
    return total.astype(bf16)


def solution(mesh):
    def per_device(attn_query, attn_key, attn_value, out_weight):
        heads = attn_query.shape[1] // HD
        form = heads_form if heads == mesh.shape["ctx"] else gather_form
        return form(attn_query, attn_key, attn_value, out_weight)

    return jax.shard_map(
        per_device,
        mesh=mesh,
        in_specs=(P("ctx", "tp"), P("ctx", "tp"), P("ctx", "tp"), P("tp", None)),
        out_specs=P("ctx", "tp"),
        check_vma=False,
    )
```

```python
import functools

import jax
import jax.numpy as jnp
from jax import lax
from jax.experimental import pallas as pl
from jax.experimental.pallas import tpu as pltpu
from jax.sharding import PartitionSpec as P

HD = 128
MIB = 1 << 20
OWN_PARTS = 2
STAT_ROWS = 16
LOG2E = 1.4426950408889634
FETCH_MIB = 40
COST = pl.CostEstimate(flops=1, bytes_accessed=1, transcendentals=1)
VMEM = pl.BlockSpec(memory_space=pltpu.VMEM)


def params(mib):
    return pltpu.CompilerParams(vmem_limit_bytes=mib * MIB)


def attend(queries, keys, values, query_pos):
    rows = queries.shape[0]
    local_heads = queries.shape[1] // HD
    scale = HD ** (-0.5)
    shaped_q = queries.reshape(rows, local_heads, HD)
    latest = jnp.max(query_pos)
    initial = (
        jnp.full((local_heads, rows), -1e30, jnp.float32),
        jnp.zeros((local_heads, rows), jnp.float32),
        jnp.zeros((local_heads, rows, HD), jnp.float32),
    )
    piece_keys = lax.all_gather(keys, "ctx", axis=0, tiled=True)
    piece_values = lax.all_gather(values, "ctx", axis=0, tiled=True)
    count_rows = piece_keys.shape[0]
    span_rows = 2 * rows

    def one_block(block, state):
        offset = block * span_rows
        block_keys = lax.dynamic_slice_in_dim(piece_keys, offset, span_rows, 0).reshape(
            span_rows, local_heads, HD
        )
        block_values = lax.dynamic_slice_in_dim(piece_values, offset, span_rows, 0).reshape(
            span_rows, local_heads, HD
        )
        key_pos = offset + jnp.arange(span_rows, dtype=jnp.int32)

        def compute(inner):
            maxes, totals, accum = inner
            scores = (
                jnp.einsum("qhd,khd->hqk", shaped_q, block_keys, preferred_element_type=jnp.float32)
                * scale
            )
            allowed = key_pos[None, None, :] <= query_pos[None, :, None]
            new_max = jnp.maximum(maxes, jnp.max(jnp.where(allowed, scores, -1e30), axis=-1))
            factor = jnp.exp(maxes - new_max)
            weights = jnp.where(allowed, jnp.exp(scores - new_max[..., None]), 0.0)
            totals = totals * factor + jnp.sum(weights, axis=-1)
            accum = accum * factor[..., None] + jnp.einsum(
                "hqk,khd->hqd",
                weights.astype(jnp.bfloat16),
                block_values,
                preferred_element_type=jnp.float32,
            )
            return (new_max, totals, accum)

        return lax.cond(jnp.min(key_pos) <= latest, compute, lambda inner: inner, state)

    maxes, totals, accum = lax.fori_loop(0, count_rows // span_rows, one_block, initial)
    result = accum / totals[..., None]
    return jnp.transpose(result, (1, 0, 2)).reshape(rows, local_heads * HD).astype(jnp.bfloat16)


def gather_form(attn_query, attn_key, attn_value, out_weight):
    rows = attn_query.shape[0]
    query_pos = lax.axis_index("ctx") * rows + jnp.arange(rows, dtype=jnp.int32)
    heads = attend(attn_query, attn_key, attn_value, query_pos)
    partial_value = jnp.dot(heads, out_weight, preferred_element_type=jnp.float32)
    return lax.psum_scatter(
        partial_value.astype(jnp.bfloat16), "tp", scatter_dimension=1, tiled=True
    )


def pack_kernel(half, me_ref, q_ref, k_ref, v_ref, *refs):
    inner, cross, (held, sem) = refs[:half], refs[half : 2 * half], refs[2 * half :]
    upper, place = me_ref[0] // half, lax.rem(me_ref[0], half)
    copies = [
        pltpu.make_async_copy(ref, held.at[part], sem.at[part])
        for part, ref in enumerate((q_ref, k_ref, v_ref))
    ]
    for one in copies:
        one.start()
    for part, one in enumerate(copies):
        one.wait()
        for shift in range(half):
            goal = place ^ shift
            cols = pl.ds(pl.multiple_of(goal * 2 * HD, 2 * HD), 2 * HD)
            inner[shift][part] = held[part, :, cols]
    for shift in range(half):
        goal = place ^ shift
        even = pl.ds(pl.multiple_of(goal * 2 * HD, HD), HD)
        odd = pl.ds(pl.multiple_of(goal * 2 * HD + HD, HD), HD)

        @pl.when(upper == 0)
        def _():
            cross[shift][0] = held[1, :, odd]
            cross[shift][1] = held[2, :, odd]

        @pl.when(upper == 1)
        def _():
            cross[shift][0] = held[0, :, even]
            cross[shift][1] = held[0, :, even]


def split3(value):
    high = value.astype(jnp.bfloat16)
    value = value - high.astype(jnp.float32)
    middle = value.astype(jnp.bfloat16)
    return high, middle, (value - middle.astype(jnp.float32)).astype(jnp.bfloat16)


def gather(half, place, rows, pieces, part, out, cols=slice(None)):
    for shift in range(half):
        source = place ^ shift
        at = pl.ds(pl.multiple_of(source * rows, rows), rows)
        out[at, :] = pieces[shift][part, :, cols]


def scores(query, keys):
    dims = (((1,), (1,)), ((), ()))
    return lax.dot_general(query, keys, dims, preferred_element_type=jnp.float32)


def weigh(raw, top, values):
    weights = jnp.exp2((raw - top) * (HD ** (-0.5) * LOG2E))
    total = jnp.sum(weights, axis=1, keepdims=True)
    acc = jnp.dot(weights.astype(jnp.bfloat16), values, preferred_element_type=jnp.float32)
    return total, acc


def log_sum(top, total):
    return top * (HD ** (-0.5) * LOG2E) + jnp.log2(total)


def inner_kernel(half, me_ref, *refs):
    inner, (o_ref, table_ref), (q_all, k_all, v_all) = refs[:half], refs[half:-3], refs[-3:]
    rows = inner[0].shape[1]
    place = lax.rem(me_ref[0], half)
    for part, out in enumerate((q_all, k_all, v_all)):
        gather(half, place, rows, inner, part, out)
    diag = lax.broadcasted_iota(jnp.int32, (rows, rows), 1) <= lax.broadcasted_iota(
        jnp.int32, (rows, rows), 0
    )
    lane = lax.broadcasted_iota(jnp.int32, (rows, HD), 1)
    table = jnp.zeros((rows, HD), jnp.float32)
    for block in reversed(range(half)):
        lo, hi = block * rows, (block + 1) * rows
        for head in range(2):
            at = slice(head * HD, (head + 1) * HD)
            query = q_all[lo:hi, at]
            last = jnp.where(diag, scores(query, k_all[lo:hi, at]), -1e30)
            top = jnp.max(last, axis=1, keepdims=True)
            if block:
                early = scores(query, k_all[0:lo, at])
                top = jnp.maximum(top, jnp.max(early, axis=1, keepdims=True))
            total, acc = weigh(last, top, v_all[lo:hi, at])
            if block:
                total_early, acc_early = weigh(early, top, v_all[0:lo, at])
                total, acc = total + total_early, acc + acc_early
            o_ref[lo:hi, at] = acc / total
            table = jnp.where(lane == head * half + block, log_sum(top, total), table)
    table_ref[...] = table


def cross_kernel(half, me_ref, *refs):
    inner, cross, (o_ref, table_ref) = refs[:half], refs[half : 2 * half], refs[2 * half : 2 * half + 2]
    back, over = refs[2 * half + 2 : 3 * half + 2], refs[3 * half + 2 : 4 * half + 2]
    q_x, k_x, v_x, o_all, o_x, stats = refs[4 * half + 2 :]
    rows = inner[0].shape[1]
    upper, place = me_ref[0] // half, lax.rem(me_ref[0], half)

    @pl.when(upper == 0)
    def _():
        gather(half, place, rows, cross, 0, q_x)
        gather(half, place, rows, inner, 1, k_x, slice(0, HD))
        gather(half, place, rows, inner, 2, v_x, slice(0, HD))

    @pl.when(upper == 1)
    def _():
        gather(half, place, rows, inner, 0, q_x, slice(HD, 2 * HD))
        gather(half, place, rows, cross, 0, k_x)
        gather(half, place, rows, cross, 1, v_x)

    lane = lax.broadcasted_iota(jnp.int32, (rows, HD), 1)
    logs = table_ref[...]
    table = logs
    for block in range(half):
        lo, hi = block * rows, (block + 1) * rows
        raw = scores(q_x[lo:hi, :], k_x[...])
        top = jnp.max(raw, axis=1, keepdims=True)
        total, acc = weigh(raw, top, v_x[...])
        result = acc / total
        o_x[lo:hi, :] = result.astype(jnp.bfloat16)
        log_x = log_sum(top, total)
        table = jnp.where(lane == half + block, log_x, table)
        gap = jnp.where(upper == 1, log_x - logs[:, half + block : half + block + 1], -1e30)
        near, far = 1.0 / (1.0 + jnp.exp2(gap)), 1.0 / (1.0 + jnp.exp2(-gap))
        o_all[lo:hi, :HD] = o_ref[lo:hi, :HD].astype(jnp.bfloat16)
        o_all[lo:hi, HD:] = (near * o_ref[lo:hi, HD:] + far * result).astype(jnp.bfloat16)
    turned = jnp.transpose(table)
    for i, part in enumerate(split3(turned[0 : 2 * half, :])):
        stats[i] = part.astype(jnp.float32)
    empty = jnp.zeros((STAT_ROWS - 3, rows), jnp.float32)
    for shift in range(half):
        goal = place ^ shift
        at = pl.ds(pl.multiple_of(goal * rows, rows), rows)
        for out, source, first in ((back[shift], o_all, 0), (over[shift], o_x, half)):
            out[0:rows, :] = source[at, :]
            lines = [stats[i, pl.ds(first + goal, 1), :] for i in range(3)]
            block = jnp.concatenate(lines + [empty], axis=0).astype(jnp.bfloat16)
            wide = out.shape[1]
            for step in range(rows // wide):
                here = slice(rows + step * STAT_ROWS, rows + (step + 1) * STAT_ROWS)
                out[here, :] = block[:, step * wide : (step + 1) * wide]


def assemble(half, me_ref, back, over, heads):
    rows = heads.shape[0]
    upper, place = me_ref[0] // half, lax.rem(me_ref[0], half)

    def read_log(piece):
        wide = piece.shape[1]
        blocks = [
            piece[rows + i * STAT_ROWS : rows + (i + 1) * STAT_ROWS, :] for i in range(rows // wide)
        ]
        block = jnp.concatenate([one.astype(jnp.float32) for one in blocks], axis=1)
        return block[0:1, :] + block[1:2, :] + block[2:3, :]

    gaps = []
    for shift in range(half):
        gap = read_log(over[shift]) - read_log(back[shift])
        gaps.append(jnp.where(upper == 1, gap, -1e30))
    table = jnp.concatenate(gaps + [jnp.zeros((HD - half, rows), jnp.float32)], axis=0)
    table = jnp.transpose(table)
    for shift in range(half):
        source = place ^ shift
        even = pl.ds(pl.multiple_of(source * 2 * HD, HD), HD)
        odd = pl.ds(pl.multiple_of(source * 2 * HD + HD, HD), HD)
        gap = table[:, shift : shift + 1]
        near = 1.0 / (1.0 + jnp.exp2(gap))
        far = 1.0 / (1.0 + jnp.exp2(-gap))
        merged = near * back[shift][0:rows, 0:HD].astype(jnp.float32)
        merged += far * over[shift][0:rows, :].astype(jnp.float32)
        heads[:, even] = merged.astype(jnp.bfloat16)
        heads[:, odd] = back[shift][0:rows, HD:]


def multiply(heads, weight, out, tile):
    for at in range(0, out.shape[1], tile):
        out[:, at : at + tile] = jnp.dot(
            heads[...], weight[:, at : at + tile], preferred_element_type=jnp.float32
        ).astype(jnp.bfloat16)


def first_kernel(half, tile, me_ref, *refs):
    back, over, (weight, heads, out) = refs[:half], refs[half : 2 * half], refs[2 * half :]
    assemble(half, me_ref, back, over, heads)
    multiply(heads, weight, out, tile)


def later_kernel(tile, heads, *refs):
    count = len(refs) // 2
    for weight, out in zip(refs[:count], refs[count:]):
        multiply(heads, weight, out, tile)


def project(heads, weights):
    out = jax.ShapeDtypeStruct((heads.shape[0], weights[0].shape[1]), jnp.bfloat16)
    return pl.pallas_call(
        functools.partial(later_kernel, 512),
        in_specs=[VMEM] * (1 + len(weights)),
        out_specs=[VMEM] * len(weights),
        out_shape=[out] * len(weights),
        compiler_params=params(16),
        cost_estimate=COST,
    )(heads, *weights)


def fetch_kernel(place_ref, w_ref, *refs):
    outs, sem = refs[:-1], refs[-1]
    cols = outs[0].shape[1]
    copies = []
    for which, out in enumerate(outs):
        at = pl.ds(pl.multiple_of(place_ref[1 + which], cols), cols)
        copies.append(pltpu.make_async_copy(w_ref.at[:, at], out, sem.at[which]))
    for one in copies:
        one.start()
    for one in copies:
        one.wait()


def fetch(place, weight, cols):
    depth, groups = weight.shape[0], place.shape[0] - 1
    return pl.pallas_call(
        fetch_kernel,
        in_specs=[pl.BlockSpec(memory_space=pltpu.SMEM), pl.BlockSpec(memory_space=pl.ANY)],
        out_specs=[VMEM] * groups,
        out_shape=[jax.ShapeDtypeStruct((depth, cols), weight.dtype)] * groups,
        scratch_shapes=[pltpu.SemaphoreType.DMA((groups,))],
        compiler_params=params(FETCH_MIB),
        cost_estimate=pl.CostEstimate(
            flops=1, bytes_accessed=4 * depth * cols * groups, transcendentals=1
        ),
    )(place, weight)


def heads_form(attn_query, attn_key, attn_value, out_weight):
    n, tp = lax.axis_size("ctx"), lax.axis_size("tp")
    half = n // 2
    rows = attn_query.shape[0]
    bf16, f32 = jnp.bfloat16, jnp.float32
    me, mine = lax.axis_index("ctx"), lax.axis_index("tp")
    place = me.astype(jnp.int32).reshape(1)
    smem = pl.BlockSpec(memory_space=pltpu.SMEM)

    def within(shift):
        return [(i, i ^ shift) for i in range(n)]

    def between(shift, lower, upper):
        up = [(i, half + (i ^ shift)) for i in range(half)]
        down = [(half + i, i ^ shift) for i in range(half)]
        return up * lower + down * upper

    inner_shape = jax.ShapeDtypeStruct((3, rows, 2 * HD), bf16)
    cross_shape = jax.ShapeDtypeStruct((2, rows, HD), bf16)
    packed = pl.pallas_call(
        functools.partial(pack_kernel, half),
        in_specs=[smem] + [pl.BlockSpec(memory_space=pl.ANY)] * 3,
        out_specs=[VMEM] * n,
        out_shape=[inner_shape] * half + [cross_shape] * half,
        scratch_shapes=[
            pltpu.VMEM((3, rows, n * HD), bf16),
            pltpu.SemaphoreType.DMA((3,)),
        ],
        compiler_params=params(56),
        cost_estimate=COST,
    )(place, attn_query, attn_key, attn_value)
    inner, cross = list(packed[:half]), list(packed[half:])

    cols = out_weight.shape[1] // tp
    planes = tp // 2
    y, core = mine // 2, lax.rem(mine, 2)
    swap = [(i, i ^ 1) for i in range(tp)]

    def wanted(plane):
        groups = [2 * plane + 1 - core, 2 * plane + core]
        return jnp.stack([me] + [group * cols for group in groups]).astype(jnp.int32)

    near = [
        fetch(wanted(lax.rem(y + shift, planes)), out_weight, cols) for shift in range(1, planes)
    ]
    for shift in range(1, half):
        inner[shift] = lax.ppermute(inner[shift], "ctx", within(shift))
    cross = [
        lax.ppermute(piece, "ctx", between(shift, 1, 1)) for shift, piece in enumerate(cross)
    ]

    inner[1], *rest = lax.optimization_barrier((inner[1], *inner[2:], near))
    inner[2:], near = rest[:-1], rest[-1]
    back_shape = jax.ShapeDtypeStruct((rows + STAT_ROWS * (rows // (2 * HD)), 2 * HD), bf16)
    over_shape = jax.ShapeDtypeStruct((rows + STAT_ROWS * (rows // HD), HD), bf16)
    big, small = pltpu.VMEM((half * rows, 2 * HD), bf16), pltpu.VMEM((half * rows, HD), bf16)
    results = pl.pallas_call(
        functools.partial(inner_kernel, half),
        in_specs=[smem] + [VMEM] * half,
        out_specs=[VMEM] * 2,
        out_shape=[
            jax.ShapeDtypeStruct((half * rows, 2 * HD), f32),
            jax.ShapeDtypeStruct((rows, HD), f32),
        ],
        scratch_shapes=[big] * 3,
        compiler_params=params(24),
        cost_estimate=COST,
    )(place, *inner)
    outs = pl.pallas_call(
        functools.partial(cross_kernel, half),
        in_specs=[smem] + [VMEM] * (n + 2),
        out_specs=[VMEM] * n,
        out_shape=[back_shape] * half + [over_shape] * half,
        scratch_shapes=[small] * 3 + [big, small, pltpu.VMEM((3, n, rows), f32)],
        compiler_params=params(24),
        cost_estimate=COST,
    )(place, *inner, *cross, *results)
    back, over = list(outs[:half]), list(outs[half:])
    over = [lax.ppermute(piece, "ctx", between(shift, 1, 0)) for shift, piece in enumerate(over)]
    for shift in range(1, half):
        back[shift] = lax.ppermute(back[shift], "ctx", within(shift))

    tied = (back[1], *over, *back[2:])
    back[1], *tied = lax.optimization_barrier(tied)
    over, back[2:] = tied[:half], tied[half:]
    heads, crossing = None, []
    for shift, (w_give, w_keep) in enumerate(near, 1):
        perm = [(i, (i + 2 * shift) % tp) for i in range(tp)]
        if heads is None:
            heads, give = pl.pallas_call(
                functools.partial(first_kernel, half, 512),
                in_specs=[smem] + [VMEM] * (n + 1),
                out_specs=[VMEM] * 2,
                out_shape=[
                    jax.ShapeDtypeStruct((rows, n * HD), bf16),
                    jax.ShapeDtypeStruct((rows, cols), bf16),
                ],
                compiler_params=params(16),
                cost_estimate=COST,
            )(place, *back, *over, w_give)
        else:
            (give,) = project(heads, [w_give])
        (keep,) = project(heads, [w_keep])
        both = (keep.astype(f32) + lax.ppermute(give, "tp", swap).astype(f32)).astype(bf16)
        crossing.append(lax.ppermute(both, "tp", perm))
        both, heads = lax.optimization_barrier((both, heads))
    out_weight, heads = lax.optimization_barrier((out_weight, heads))
    give, keep = project(heads, fetch(wanted(y), out_weight, cols))
    piece = cols // OWN_PARTS
    swapped = [
        lax.ppermute(give[:, at : at + piece], "tp", swap) for at in range(0, cols, piece)
    ]
    total = keep.astype(f32) + jnp.concatenate(swapped, axis=1).astype(f32)
    for one in crossing:
        total += one.astype(f32)
    return total.astype(bf16)


def solution(mesh):
    def per_device(attn_query, attn_key, attn_value, out_weight):
        heads, n, tp = attn_query.shape[1] // HD, mesh.shape["ctx"], mesh.shape["tp"]
        paired = heads == n and n > 2 and n & (n - 1) == 0 and n <= HD and tp % 2 == 0 and tp > 2
        form = heads_form if paired and attn_query.shape[0] % (2 * HD) == 0 else gather_form
        return form(attn_query, attn_key, attn_value, out_weight)

    return jax.shard_map(
        per_device,
        mesh=mesh,
        in_specs=(P("ctx", "tp"), P("ctx", "tp"), P("ctx", "tp"), P("tp", None)),
        out_specs=P("ctx", "tp"),
        check_vma=False,
    )
```

```python
import functools

import jax
import jax.numpy as jnp
from jax import lax
from jax.experimental import pallas as pl
from jax.experimental.pallas import tpu as pltpu
from jax.sharding import PartitionSpec as P

HD = 128
MIB = 1 << 20
OWN_PARTS = 2
STAT_ROWS = 16
T2TIE = (2, 3)
LOG2E = 1.4426950408889634
FETCH_MIB = 40
COST = pl.CostEstimate(flops=1, bytes_accessed=1, transcendentals=1)
VMEM = pl.BlockSpec(memory_space=pltpu.VMEM)


def params(mib):
    return pltpu.CompilerParams(vmem_limit_bytes=mib * MIB)


def attend(queries, keys, values, query_pos):
    rows = queries.shape[0]
    local_heads = queries.shape[1] // HD
    scale = HD ** (-0.5)
    shaped_q = queries.reshape(rows, local_heads, HD)
    latest = jnp.max(query_pos)
    initial = (
        jnp.full((local_heads, rows), -1e30, jnp.float32),
        jnp.zeros((local_heads, rows), jnp.float32),
        jnp.zeros((local_heads, rows, HD), jnp.float32),
    )
    piece_keys = lax.all_gather(keys, "ctx", axis=0, tiled=True)
    piece_values = lax.all_gather(values, "ctx", axis=0, tiled=True)
    count_rows = piece_keys.shape[0]
    span_rows = 2 * rows

    def one_block(block, state):
        offset = block * span_rows
        block_keys = lax.dynamic_slice_in_dim(piece_keys, offset, span_rows, 0).reshape(
            span_rows, local_heads, HD
        )
        block_values = lax.dynamic_slice_in_dim(piece_values, offset, span_rows, 0).reshape(
            span_rows, local_heads, HD
        )
        key_pos = offset + jnp.arange(span_rows, dtype=jnp.int32)

        def compute(inner):
            maxes, totals, accum = inner
            scores = (
                jnp.einsum("qhd,khd->hqk", shaped_q, block_keys, preferred_element_type=jnp.float32)
                * scale
            )
            allowed = key_pos[None, None, :] <= query_pos[None, :, None]
            new_max = jnp.maximum(maxes, jnp.max(jnp.where(allowed, scores, -1e30), axis=-1))
            factor = jnp.exp(maxes - new_max)
            weights = jnp.where(allowed, jnp.exp(scores - new_max[..., None]), 0.0)
            totals = totals * factor + jnp.sum(weights, axis=-1)
            accum = accum * factor[..., None] + jnp.einsum(
                "hqk,khd->hqd",
                weights.astype(jnp.bfloat16),
                block_values,
                preferred_element_type=jnp.float32,
            )
            return (new_max, totals, accum)

        return lax.cond(jnp.min(key_pos) <= latest, compute, lambda inner: inner, state)

    maxes, totals, accum = lax.fori_loop(0, count_rows // span_rows, one_block, initial)
    result = accum / totals[..., None]
    return jnp.transpose(result, (1, 0, 2)).reshape(rows, local_heads * HD).astype(jnp.bfloat16)


def gather_form(attn_query, attn_key, attn_value, out_weight):
    rows = attn_query.shape[0]
    query_pos = lax.axis_index("ctx") * rows + jnp.arange(rows, dtype=jnp.int32)
    heads = attend(attn_query, attn_key, attn_value, query_pos)
    partial_value = jnp.dot(heads, out_weight, preferred_element_type=jnp.float32)
    return lax.psum_scatter(
        partial_value.astype(jnp.bfloat16), "tp", scatter_dimension=1, tiled=True
    )


def pack_kernel(half, me_ref, q_ref, k_ref, v_ref, *refs):
    inner, cross, (held, sem) = refs[:half], refs[half : 2 * half], refs[2 * half :]
    upper, place = me_ref[0] // half, lax.rem(me_ref[0], half)
    copies = [
        pltpu.make_async_copy(ref, held.at[part], sem.at[part])
        for part, ref in enumerate((q_ref, k_ref, v_ref))
    ]
    for one in copies:
        one.start()
    for part, one in enumerate(copies):
        one.wait()
        for shift in range(half):
            goal = place ^ shift
            cols = pl.ds(pl.multiple_of(goal * 2 * HD, 2 * HD), 2 * HD)
            inner[shift][part] = held[part, :, cols]
    for shift in range(half):
        goal = place ^ shift
        even = pl.ds(pl.multiple_of(goal * 2 * HD, HD), HD)
        odd = pl.ds(pl.multiple_of(goal * 2 * HD + HD, HD), HD)

        @pl.when(upper == 0)
        def _():
            cross[shift][0] = held[1, :, odd]
            cross[shift][1] = held[2, :, odd]

        @pl.when(upper == 1)
        def _():
            cross[shift][0] = held[0, :, even]
            cross[shift][1] = held[0, :, even]


def split3(value):
    high = value.astype(jnp.bfloat16)
    value = value - high.astype(jnp.float32)
    middle = value.astype(jnp.bfloat16)
    return high, middle, (value - middle.astype(jnp.float32)).astype(jnp.bfloat16)


def gather(half, place, rows, pieces, part, out, cols=slice(None)):
    for shift in range(half):
        source = place ^ shift
        at = pl.ds(pl.multiple_of(source * rows, rows), rows)
        out[at, :] = pieces[shift][part, :, cols]


def scores(query, keys):
    dims = (((1,), (1,)), ((), ()))
    return lax.dot_general(query, keys, dims, preferred_element_type=jnp.float32)


def weigh(raw, top, values):
    weights = jnp.exp2((raw - top) * (HD ** (-0.5) * LOG2E))
    total = jnp.sum(weights, axis=1, keepdims=True)
    acc = jnp.dot(weights.astype(jnp.bfloat16), values, preferred_element_type=jnp.float32)
    return total, acc


def log_sum(top, total):
    return top * (HD ** (-0.5) * LOG2E) + jnp.log2(total)


def inner_kernel(half, me_ref, *refs):
    inner, (o_ref, table_ref), (q_all, k_all, v_all) = refs[:half], refs[half:-3], refs[-3:]
    rows = inner[0].shape[1]
    place = lax.rem(me_ref[0], half)
    for part, out in enumerate((q_all, k_all, v_all)):
        gather(half, place, rows, inner, part, out)
    diag = lax.broadcasted_iota(jnp.int32, (rows, rows), 1) <= lax.broadcasted_iota(
        jnp.int32, (rows, rows), 0
    )
    lane = lax.broadcasted_iota(jnp.int32, (rows, HD), 1)
    table = jnp.zeros((rows, HD), jnp.float32)
    for block in reversed(range(half)):
        lo, hi = block * rows, (block + 1) * rows
        for head in range(2):
            at = slice(head * HD, (head + 1) * HD)
            query = q_all[lo:hi, at]
            last = jnp.where(diag, scores(query, k_all[lo:hi, at]), -1e30)
            top = jnp.max(last, axis=1, keepdims=True)
            if block:
                early = scores(query, k_all[0:lo, at])
                top = jnp.maximum(top, jnp.max(early, axis=1, keepdims=True))
            total, acc = weigh(last, top, v_all[lo:hi, at])
            if block:
                total_early, acc_early = weigh(early, top, v_all[0:lo, at])
                total, acc = total + total_early, acc + acc_early
            o_ref[lo:hi, at] = acc / total
            table = jnp.where(lane == head * half + block, log_sum(top, total), table)
    table_ref[...] = table


def cross_kernel(half, me_ref, *refs):
    inner, cross, (o_ref, table_ref) = refs[:half], refs[half : 2 * half], refs[2 * half : 2 * half + 2]
    back, over = refs[2 * half + 2 : 3 * half + 2], refs[3 * half + 2 : 4 * half + 2]
    q_x, k_x, v_x, o_all, o_x, stats = refs[4 * half + 2 :]
    rows = inner[0].shape[1]
    upper, place = me_ref[0] // half, lax.rem(me_ref[0], half)

    @pl.when(upper == 0)
    def _():
        gather(half, place, rows, cross, 0, q_x)
        gather(half, place, rows, inner, 1, k_x, slice(0, HD))
        gather(half, place, rows, inner, 2, v_x, slice(0, HD))

    @pl.when(upper == 1)
    def _():
        gather(half, place, rows, inner, 0, q_x, slice(HD, 2 * HD))
        gather(half, place, rows, cross, 0, k_x)
        gather(half, place, rows, cross, 1, v_x)

    lane = lax.broadcasted_iota(jnp.int32, (rows, HD), 1)
    logs = table_ref[...]
    table = logs
    for block in range(half):
        lo, hi = block * rows, (block + 1) * rows
        raw = scores(q_x[lo:hi, :], k_x[...])
        top = jnp.max(raw, axis=1, keepdims=True)
        total, acc = weigh(raw, top, v_x[...])
        result = acc / total
        o_x[lo:hi, :] = result.astype(jnp.bfloat16)
        log_x = log_sum(top, total)
        table = jnp.where(lane == half + block, log_x, table)
        gap = jnp.where(upper == 1, log_x - logs[:, half + block : half + block + 1], -1e30)
        near, far = 1.0 / (1.0 + jnp.exp2(gap)), 1.0 / (1.0 + jnp.exp2(-gap))
        o_all[lo:hi, :HD] = o_ref[lo:hi, :HD].astype(jnp.bfloat16)
        o_all[lo:hi, HD:] = (near * o_ref[lo:hi, HD:] + far * result).astype(jnp.bfloat16)
    turned = jnp.transpose(table)
    for i, part in enumerate(split3(turned[0 : 2 * half, :])):
        stats[i] = part.astype(jnp.float32)
    for shift in range(half):
        goal = place ^ shift
        at = pl.ds(pl.multiple_of(goal * rows, rows), rows)
        for out, source, first in ((back[shift], o_all, 0), (over[shift], o_x, half)):
            out[0:rows, :] = source[at, :]
            wide = out.shape[1]
            lines = [stats[i, pl.ds(first + goal, 1), :] for i in range(3)]
            lines = [line[:, at : at + wide] for line in lines for at in range(0, rows, wide)]
            empty = jnp.zeros((STAT_ROWS - len(lines), wide), jnp.float32)
            out[rows:, :] = jnp.concatenate(lines + [empty], axis=0).astype(jnp.bfloat16)


def assemble(half, me_ref, back, over, heads):
    rows = heads.shape[0]
    upper, place = me_ref[0] // half, lax.rem(me_ref[0], half)

    def read_log(piece):
        steps = rows // piece.shape[1]
        block = piece[rows:, :].astype(jnp.float32)
        sums = [
            block[i : i + 1, :] + block[steps + i : steps + i + 1, :]
            + block[2 * steps + i : 2 * steps + i + 1, :]
            for i in range(steps)
        ]
        return jnp.concatenate(sums, axis=1)

    gaps = []
    for shift in range(half):
        gap = read_log(over[shift]) - read_log(back[shift])
        gaps.append(jnp.where(upper == 1, gap, -1e30))
    table = jnp.concatenate(gaps + [jnp.zeros((HD - half, rows), jnp.float32)], axis=0)
    table = jnp.transpose(table)
    for shift in range(half):
        source = place ^ shift
        even = pl.ds(pl.multiple_of(source * 2 * HD, HD), HD)
        odd = pl.ds(pl.multiple_of(source * 2 * HD + HD, HD), HD)
        gap = table[:, shift : shift + 1]
        near = 1.0 / (1.0 + jnp.exp2(gap))
        far = 1.0 / (1.0 + jnp.exp2(-gap))
        merged = near * back[shift][0:rows, 0:HD].astype(jnp.float32)
        merged += far * over[shift][0:rows, :].astype(jnp.float32)
        heads[:, even] = merged.astype(jnp.bfloat16)
        heads[:, odd] = back[shift][0:rows, HD:]


def multiply(heads, weight, out, tile):
    for at in range(0, out.shape[1], tile):
        out[:, at : at + tile] = jnp.dot(
            heads[...], weight[:, at : at + tile], preferred_element_type=jnp.float32
        ).astype(jnp.bfloat16)


def first_kernel(half, tile, me_ref, *refs):
    back, over, (weight, heads, out) = refs[:half], refs[half : 2 * half], refs[2 * half :]
    assemble(half, me_ref, back, over, heads)
    multiply(heads, weight, out, tile)


def later_kernel(tile, heads, *refs):
    count = len(refs) // 2
    for weight, out in zip(refs[:count], refs[count:]):
        multiply(heads, weight, out, tile)


def project(heads, weights):
    out = jax.ShapeDtypeStruct((heads.shape[0], weights[0].shape[1]), jnp.bfloat16)
    return pl.pallas_call(
        functools.partial(later_kernel, 512),
        in_specs=[VMEM] * (1 + len(weights)),
        out_specs=[VMEM] * len(weights),
        out_shape=[out] * len(weights),
        compiler_params=params(16),
        cost_estimate=COST,
    )(heads, *weights)


def fetch_kernel(place_ref, w_ref, *refs):
    outs, sem = refs[:-1], refs[-1]
    cols = outs[0].shape[1]
    copies = []
    for which, out in enumerate(outs):
        at = pl.ds(pl.multiple_of(place_ref[1 + which], cols), cols)
        copies.append(pltpu.make_async_copy(w_ref.at[:, at], out, sem.at[which]))
    for one in copies:
        one.start()
    for one in copies:
        one.wait()


def fetch(place, weight, cols):
    depth, groups = weight.shape[0], place.shape[0] - 1
    return pl.pallas_call(
        fetch_kernel,
        in_specs=[pl.BlockSpec(memory_space=pltpu.SMEM), pl.BlockSpec(memory_space=pl.ANY)],
        out_specs=[VMEM] * groups,
        out_shape=[jax.ShapeDtypeStruct((depth, cols), weight.dtype)] * groups,
        scratch_shapes=[pltpu.SemaphoreType.DMA((groups,))],
        compiler_params=params(FETCH_MIB),
        cost_estimate=pl.CostEstimate(
            flops=1, bytes_accessed=4 * depth * cols * groups, transcendentals=1
        ),
    )(place, weight)


def heads_form(attn_query, attn_key, attn_value, out_weight):
    n, tp = lax.axis_size("ctx"), lax.axis_size("tp")
    half = n // 2
    rows = attn_query.shape[0]
    bf16, f32 = jnp.bfloat16, jnp.float32
    me, mine = lax.axis_index("ctx"), lax.axis_index("tp")
    place = me.astype(jnp.int32).reshape(1)
    smem = pl.BlockSpec(memory_space=pltpu.SMEM)

    def within(shift):
        return [(i, i ^ shift) for i in range(n)]

    def between(shift, lower, upper):
        up = [(i, half + (i ^ shift)) for i in range(half)]
        down = [(half + i, i ^ shift) for i in range(half)]
        return up * lower + down * upper

    inner_shape = jax.ShapeDtypeStruct((3, rows, 2 * HD), bf16)
    cross_shape = jax.ShapeDtypeStruct((2, rows, HD), bf16)
    packed = pl.pallas_call(
        functools.partial(pack_kernel, half),
        in_specs=[smem] + [pl.BlockSpec(memory_space=pl.ANY)] * 3,
        out_specs=[VMEM] * n,
        out_shape=[inner_shape] * half + [cross_shape] * half,
        scratch_shapes=[
            pltpu.VMEM((3, rows, n * HD), bf16),
            pltpu.SemaphoreType.DMA((3,)),
        ],
        compiler_params=params(56),
        cost_estimate=COST,
    )(place, attn_query, attn_key, attn_value)
    inner, cross = list(packed[:half]), list(packed[half:])

    cols = out_weight.shape[1] // tp
    planes = tp // 2
    y, core = mine // 2, lax.rem(mine, 2)
    swap = [(i, i ^ 1) for i in range(tp)]

    def wanted(plane):
        groups = [2 * plane + 1 - core, 2 * plane + core]
        return jnp.stack([me] + [group * cols for group in groups]).astype(jnp.int32)

    near = [
        fetch(wanted(lax.rem(y + shift, planes)), out_weight, cols) for shift in range(1, planes)
    ]
    for shift in range(1, half):
        inner[shift] = lax.ppermute(inner[shift], "ctx", within(shift))
    cross = [
        lax.ppermute(piece, "ctx", between(shift, 1, 1)) for shift, piece in enumerate(cross)
    ]

    inner[1], *rest = lax.optimization_barrier((inner[1], *inner[2:], near))
    inner[2:], near = rest[:-1], rest[-1]
    back_shape = jax.ShapeDtypeStruct((rows + STAT_ROWS, 2 * HD), bf16)
    over_shape = jax.ShapeDtypeStruct((rows + STAT_ROWS, HD), bf16)
    big, small = pltpu.VMEM((half * rows, 2 * HD), bf16), pltpu.VMEM((half * rows, HD), bf16)
    results = pl.pallas_call(
        functools.partial(inner_kernel, half),
        in_specs=[smem] + [VMEM] * half,
        out_specs=[VMEM] * 2,
        out_shape=[
            jax.ShapeDtypeStruct((half * rows, 2 * HD), f32),
            jax.ShapeDtypeStruct((rows, HD), f32),
        ],
        scratch_shapes=[big] * 3,
        compiler_params=params(24),
        cost_estimate=COST,
    )(place, *inner)
    outs = pl.pallas_call(
        functools.partial(cross_kernel, half),
        in_specs=[smem] + [VMEM] * (n + 2),
        out_specs=[VMEM] * n,
        out_shape=[back_shape] * half + [over_shape] * half,
        scratch_shapes=[small] * 3 + [big, small, pltpu.VMEM((3, n, rows), f32)],
        compiler_params=params(24),
        cost_estimate=COST,
    )(place, *inner, *cross, *results)
    back, over = list(outs[:half]), list(outs[half:])
    for shift in range(1, half):
        back[shift] = lax.ppermute(back[shift], "ctx", within(shift))
    for shift in range(half):
        if shift in T2TIE:
            over[shift], back[1] = lax.optimization_barrier((over[shift], back[1]))
        over[shift] = lax.ppermute(over[shift], "ctx", between(shift, 1, 0))

    tied = (back[1], *over, *back[2:])
    back[1], *tied = lax.optimization_barrier(tied)
    over, back[2:] = tied[:half], tied[half:]
    heads, crossing = None, []
    for shift, (w_give, w_keep) in enumerate(near, 1):
        perm = [(i, (i + 2 * shift) % tp) for i in range(tp)]
        if heads is None:
            heads, give = pl.pallas_call(
                functools.partial(first_kernel, half, 512),
                in_specs=[smem] + [VMEM] * (n + 1),
                out_specs=[VMEM] * 2,
                out_shape=[
                    jax.ShapeDtypeStruct((rows, n * HD), bf16),
                    jax.ShapeDtypeStruct((rows, cols), bf16),
                ],
                compiler_params=params(16),
                cost_estimate=COST,
            )(place, *back, *over, w_give)
        else:
            (give,) = project(heads, [w_give])
        (keep,) = project(heads, [w_keep])
        both = (keep.astype(f32) + lax.ppermute(give, "tp", swap).astype(f32)).astype(bf16)
        crossing.append(lax.ppermute(both, "tp", perm))
        both, heads = lax.optimization_barrier((both, heads))
    out_weight, heads = lax.optimization_barrier((out_weight, heads))
    give, keep = project(heads, fetch(wanted(y), out_weight, cols))
    piece = cols // OWN_PARTS
    swapped = [
        lax.ppermute(give[:, at : at + piece], "tp", swap) for at in range(0, cols, piece)
    ]
    total = keep.astype(f32) + jnp.concatenate(swapped, axis=1).astype(f32)
    for one in crossing:
        total += one.astype(f32)
    return total.astype(bf16)


def solution(mesh):
    def per_device(attn_query, attn_key, attn_value, out_weight):
        heads, n, tp = attn_query.shape[1] // HD, mesh.shape["ctx"], mesh.shape["tp"]
        paired = heads == n and n > 2 and n & (n - 1) == 0 and n <= HD and tp % 2 == 0 and tp > 2
        form = heads_form if paired and attn_query.shape[0] == 2 * HD else gather_form
        return form(attn_query, attn_key, attn_value, out_weight)

    return jax.shard_map(
        per_device,
        mesh=mesh,
        in_specs=(P("ctx", "tp"), P("ctx", "tp"), P("ctx", "tp"), P("tp", None)),
        out_specs=P("ctx", "tp"),
        check_vma=False,
    )
```

```python
import functools

import jax
import jax.numpy as jnp
from jax import lax
from jax.experimental import pallas as pl
from jax.experimental.pallas import tpu as pltpu
from jax.sharding import PartitionSpec as P

HD = 128
MIB = 1 << 20
OWN_PARTS = 2
STEPS = 4
STAT_ROWS = 16
T2TIE = (2, 3)
LOG2E = 1.4426950408889634
FETCH_MIB = 40
COST = pl.CostEstimate(flops=1, bytes_accessed=1, transcendentals=1)
VMEM = pl.BlockSpec(memory_space=pltpu.VMEM)


def params(mib):
    return pltpu.CompilerParams(vmem_limit_bytes=mib * MIB)


def attend(queries, keys, values, query_pos):
    rows = queries.shape[0]
    local_heads = queries.shape[1] // HD
    scale = HD ** (-0.5)
    shaped_q = queries.reshape(rows, local_heads, HD)
    latest = jnp.max(query_pos)
    initial = (
        jnp.full((local_heads, rows), -1e30, jnp.float32),
        jnp.zeros((local_heads, rows), jnp.float32),
        jnp.zeros((local_heads, rows, HD), jnp.float32),
    )
    piece_keys = lax.all_gather(keys, "ctx", axis=0, tiled=True)
    piece_values = lax.all_gather(values, "ctx", axis=0, tiled=True)
    count_rows = piece_keys.shape[0]
    span_rows = 2 * rows

    def one_block(block, state):
        offset = block * span_rows
        block_keys = lax.dynamic_slice_in_dim(piece_keys, offset, span_rows, 0).reshape(
            span_rows, local_heads, HD
        )
        block_values = lax.dynamic_slice_in_dim(piece_values, offset, span_rows, 0).reshape(
            span_rows, local_heads, HD
        )
        key_pos = offset + jnp.arange(span_rows, dtype=jnp.int32)

        def compute(inner):
            maxes, totals, accum = inner
            scores = (
                jnp.einsum("qhd,khd->hqk", shaped_q, block_keys, preferred_element_type=jnp.float32)
                * scale
            )
            allowed = key_pos[None, None, :] <= query_pos[None, :, None]
            new_max = jnp.maximum(maxes, jnp.max(jnp.where(allowed, scores, -1e30), axis=-1))
            factor = jnp.exp(maxes - new_max)
            weights = jnp.where(allowed, jnp.exp(scores - new_max[..., None]), 0.0)
            totals = totals * factor + jnp.sum(weights, axis=-1)
            accum = accum * factor[..., None] + jnp.einsum(
                "hqk,khd->hqd",
                weights.astype(jnp.bfloat16),
                block_values,
                preferred_element_type=jnp.float32,
            )
            return (new_max, totals, accum)

        return lax.cond(jnp.min(key_pos) <= latest, compute, lambda inner: inner, state)

    maxes, totals, accum = lax.fori_loop(0, count_rows // span_rows, one_block, initial)
    result = accum / totals[..., None]
    return jnp.transpose(result, (1, 0, 2)).reshape(rows, local_heads * HD).astype(jnp.bfloat16)


def gather_form(attn_query, attn_key, attn_value, out_weight):
    rows = attn_query.shape[0]
    query_pos = lax.axis_index("ctx") * rows + jnp.arange(rows, dtype=jnp.int32)
    heads = attend(attn_query, attn_key, attn_value, query_pos)
    partial_value = jnp.dot(heads, out_weight, preferred_element_type=jnp.float32)
    return lax.psum_scatter(
        partial_value.astype(jnp.bfloat16), "tp", scatter_dimension=1, tiled=True
    )


def pack_kernel(half, me_ref, q_ref, k_ref, v_ref, *refs):
    inner, cross, (held, sem) = refs[:half], refs[half : 2 * half], refs[2 * half :]
    upper, place = me_ref[0] // half, lax.rem(me_ref[0], half)
    copies = [
        pltpu.make_async_copy(ref, held.at[part], sem.at[part])
        for part, ref in enumerate((q_ref, k_ref, v_ref))
    ]
    for one in copies:
        one.start()
    for part, one in enumerate(copies):
        one.wait()
        for shift in range(half):
            goal = place ^ shift
            cols = pl.ds(pl.multiple_of(goal * 2 * HD, 2 * HD), 2 * HD)
            inner[shift][part] = held[part, :, cols]
    for shift in range(half):
        goal = place ^ shift
        even = pl.ds(pl.multiple_of(goal * 2 * HD, HD), HD)
        odd = pl.ds(pl.multiple_of(goal * 2 * HD + HD, HD), HD)

        @pl.when(upper == 0)
        def _():
            cross[shift][0] = held[1, :, odd]
            cross[shift][1] = held[2, :, odd]

        @pl.when(upper == 1)
        def _():
            cross[shift][0] = held[0, :, even]
            cross[shift][1] = held[0, :, even]


def split3(value):
    high = value.astype(jnp.bfloat16)
    value = value - high.astype(jnp.float32)
    middle = value.astype(jnp.bfloat16)
    return high, middle, (value - middle.astype(jnp.float32)).astype(jnp.bfloat16)


def gather(half, place, rows, pieces, part, out, cols=slice(None)):
    for shift in range(half):
        source = place ^ shift
        at = pl.ds(pl.multiple_of(source * rows, rows), rows)
        out[at, :] = pieces[shift][part, :, cols]


def scores(query, keys):
    dims = (((1,), (1,)), ((), ()))
    return lax.dot_general(query, keys, dims, preferred_element_type=jnp.float32)


def weigh(raw, top, values):
    weights = jnp.exp2((raw - top) * (HD ** (-0.5) * LOG2E))
    total = jnp.sum(weights, axis=1, keepdims=True)
    acc = jnp.dot(weights.astype(jnp.bfloat16), values, preferred_element_type=jnp.float32)
    return total, acc


def log_sum(top, total):
    return top * (HD ** (-0.5) * LOG2E) + jnp.log2(total)


def inner_kernel(half, me_ref, *refs):
    inner, (o_ref, table_ref), (q_all, k_all, v_all) = refs[:half], refs[half:-3], refs[-3:]
    rows = inner[0].shape[1]
    place = lax.rem(me_ref[0], half)
    for part, out in enumerate((q_all, k_all, v_all)):
        gather(half, place, rows, inner, part, out)
    diag = lax.broadcasted_iota(jnp.int32, (rows, rows), 1) <= lax.broadcasted_iota(
        jnp.int32, (rows, rows), 0
    )
    lane = lax.broadcasted_iota(jnp.int32, (rows, HD), 1)
    table = jnp.zeros((rows, HD), jnp.float32)
    for block in reversed(range(half)):
        lo, hi = block * rows, (block + 1) * rows
        for head in range(2):
            at = slice(head * HD, (head + 1) * HD)
            query = q_all[lo:hi, at]
            last = jnp.where(diag, scores(query, k_all[lo:hi, at]), -1e30)
            top = jnp.max(last, axis=1, keepdims=True)
            if block:
                early = scores(query, k_all[0:lo, at])
                top = jnp.maximum(top, jnp.max(early, axis=1, keepdims=True))
            total, acc = weigh(last, top, v_all[lo:hi, at])
            if block:
                total_early, acc_early = weigh(early, top, v_all[0:lo, at])
                total, acc = total + total_early, acc + acc_early
            o_ref[lo:hi, at] = acc / total
            table = jnp.where(lane == head * half + block, log_sum(top, total), table)
    table_ref[...] = table


def cross_kernel(half, me_ref, *refs):
    inner, cross, (o_ref, table_ref) = refs[:half], refs[half : 2 * half], refs[2 * half : 2 * half + 2]
    back, over = refs[2 * half + 2 : 3 * half + 2], refs[3 * half + 2 : 4 * half + 2]
    q_x, k_x, v_x, o_all, o_x, stats = refs[4 * half + 2 :]
    rows = inner[0].shape[1]
    upper, place = me_ref[0] // half, lax.rem(me_ref[0], half)

    @pl.when(upper == 0)
    def _():
        gather(half, place, rows, cross, 0, q_x)
        gather(half, place, rows, inner, 1, k_x, slice(0, HD))
        gather(half, place, rows, inner, 2, v_x, slice(0, HD))

    @pl.when(upper == 1)
    def _():
        gather(half, place, rows, inner, 0, q_x, slice(HD, 2 * HD))
        gather(half, place, rows, cross, 0, k_x)
        gather(half, place, rows, cross, 1, v_x)

    lane = lax.broadcasted_iota(jnp.int32, (rows, HD), 1)
    logs = table_ref[...]
    table = logs
    for block in range(half):
        lo, hi = block * rows, (block + 1) * rows
        raw = scores(q_x[lo:hi, :], k_x[...])
        top = jnp.max(raw, axis=1, keepdims=True)
        total, acc = weigh(raw, top, v_x[...])
        result = acc / total
        o_x[lo:hi, :] = result.astype(jnp.bfloat16)
        log_x = log_sum(top, total)
        table = jnp.where(lane == half + block, log_x, table)
        gap = jnp.where(upper == 1, log_x - logs[:, half + block : half + block + 1], -1e30)
        near, far = 1.0 / (1.0 + jnp.exp2(gap)), 1.0 / (1.0 + jnp.exp2(-gap))
        o_all[lo:hi, :HD] = o_ref[lo:hi, :HD].astype(jnp.bfloat16)
        o_all[lo:hi, HD:] = (near * o_ref[lo:hi, HD:] + far * result).astype(jnp.bfloat16)
    turned = jnp.transpose(table)
    for i, part in enumerate(split3(turned[0 : 2 * half, :])):
        stats[i] = part.astype(jnp.float32)
    for shift in range(half):
        goal = place ^ shift
        at = pl.ds(pl.multiple_of(goal * rows, rows), rows)
        for out, source, first in ((back[shift], o_all, 0), (over[shift], o_x, half)):
            out[0:rows, :] = source[at, :]
            wide = out.shape[1]
            lines = [stats[i, pl.ds(first + goal, 1), :] for i in range(3)]
            lines = [line[:, at : at + wide] for line in lines for at in range(0, rows, wide)]
            empty = jnp.zeros((STAT_ROWS - len(lines), wide), jnp.float32)
            out[rows:, :] = jnp.concatenate(lines + [empty], axis=0).astype(jnp.bfloat16)


def assemble(half, me_ref, back, over, heads):
    rows = heads.shape[0]
    upper, place = me_ref[0] // half, lax.rem(me_ref[0], half)

    def read_log(piece):
        steps = rows // piece.shape[1]
        block = piece[rows:, :].astype(jnp.float32)
        sums = [
            block[i : i + 1, :] + block[steps + i : steps + i + 1, :]
            + block[2 * steps + i : 2 * steps + i + 1, :]
            for i in range(steps)
        ]
        return jnp.concatenate(sums, axis=1)

    gaps = []
    for shift in range(half):
        gap = read_log(over[shift]) - read_log(back[shift])
        gaps.append(jnp.where(upper == 1, gap, -1e30))
    table = jnp.concatenate(gaps + [jnp.zeros((HD - half, rows), jnp.float32)], axis=0)
    table = jnp.transpose(table)
    for shift in range(half):
        source = place ^ shift
        even = pl.ds(pl.multiple_of(source * 2 * HD, HD), HD)
        odd = pl.ds(pl.multiple_of(source * 2 * HD + HD, HD), HD)
        gap = table[:, shift : shift + 1]
        near = 1.0 / (1.0 + jnp.exp2(gap))
        far = 1.0 / (1.0 + jnp.exp2(-gap))
        merged = near * back[shift][0:rows, 0:HD].astype(jnp.float32)
        merged += far * over[shift][0:rows, :].astype(jnp.float32)
        heads[:, even] = merged.astype(jnp.bfloat16)
        heads[:, odd] = back[shift][0:rows, HD:]


def multiply(heads, weight, out, tile):
    for at in range(0, out.shape[1], tile):
        out[:, at : at + tile] = jnp.dot(
            heads[...], weight[:, at : at + tile], preferred_element_type=jnp.float32
        ).astype(jnp.bfloat16)


def first_kernel(half, tile, me_ref, *refs):
    back, over, (weight, heads, out) = refs[:half], refs[half : 2 * half], refs[2 * half :]
    assemble(half, me_ref, back, over, heads)
    multiply(heads, weight, out, tile)


def later_kernel(tile, heads, *refs):
    count = len(refs) // 2
    for weight, out in zip(refs[:count], refs[count:]):
        multiply(heads, weight, out, tile)


def last_kernel(keep, *refs):
    swapped, (whole, out, held, sem) = refs[:OWN_PARTS], refs[OWN_PARTS:]
    rows, cols = keep.shape
    step, wide = rows // STEPS, cols // OWN_PARTS
    copies = []
    for i in range(STEPS):
        at = slice(i * step, (i + 1) * step)
        for j, part in enumerate(swapped):
            here = slice(j * wide, (j + 1) * wide)
            total = keep[at, here].astype(jnp.float32) + part[at, :].astype(jnp.float32)
            held[at, here] = (total + whole[at, here].astype(jnp.float32)).astype(jnp.bfloat16)
        rows_at = pl.ds(i * step, step)
        copies.append(pltpu.make_async_copy(held.at[rows_at], out.at[rows_at], sem.at[i]))
        copies[-1].start()
    for one in copies:
        one.wait()


def project(heads, weights):
    out = jax.ShapeDtypeStruct((heads.shape[0], weights[0].shape[1]), jnp.bfloat16)
    return pl.pallas_call(
        functools.partial(later_kernel, 512),
        in_specs=[VMEM] * (1 + len(weights)),
        out_specs=[VMEM] * len(weights),
        out_shape=[out] * len(weights),
        compiler_params=params(16),
        cost_estimate=COST,
    )(heads, *weights)


def fetch_kernel(place_ref, w_ref, *refs):
    outs, sem = refs[:-1], refs[-1]
    cols = outs[0].shape[1]
    copies = []
    for which, out in enumerate(outs):
        at = pl.ds(pl.multiple_of(place_ref[1 + which], cols), cols)
        copies.append(pltpu.make_async_copy(w_ref.at[:, at], out, sem.at[which]))
    for one in copies:
        one.start()
    for one in copies:
        one.wait()


def fetch(place, weight, cols):
    depth, groups = weight.shape[0], place.shape[0] - 1
    return pl.pallas_call(
        fetch_kernel,
        in_specs=[pl.BlockSpec(memory_space=pltpu.SMEM), pl.BlockSpec(memory_space=pl.ANY)],
        out_specs=[VMEM] * groups,
        out_shape=[jax.ShapeDtypeStruct((depth, cols), weight.dtype)] * groups,
        scratch_shapes=[pltpu.SemaphoreType.DMA((groups,))],
        compiler_params=params(FETCH_MIB),
        cost_estimate=pl.CostEstimate(
            flops=1, bytes_accessed=4 * depth * cols * groups, transcendentals=1
        ),
    )(place, weight)


def heads_form(attn_query, attn_key, attn_value, out_weight):
    n, tp = lax.axis_size("ctx"), lax.axis_size("tp")
    half = n // 2
    rows = attn_query.shape[0]
    bf16, f32 = jnp.bfloat16, jnp.float32
    me, mine = lax.axis_index("ctx"), lax.axis_index("tp")
    place = me.astype(jnp.int32).reshape(1)
    smem = pl.BlockSpec(memory_space=pltpu.SMEM)

    def within(shift):
        return [(i, i ^ shift) for i in range(n)]

    def between(shift, lower, upper):
        up = [(i, half + (i ^ shift)) for i in range(half)]
        down = [(half + i, i ^ shift) for i in range(half)]
        return up * lower + down * upper

    inner_shape = jax.ShapeDtypeStruct((3, rows, 2 * HD), bf16)
    cross_shape = jax.ShapeDtypeStruct((2, rows, HD), bf16)
    packed = pl.pallas_call(
        functools.partial(pack_kernel, half),
        in_specs=[smem] + [pl.BlockSpec(memory_space=pl.ANY)] * 3,
        out_specs=[VMEM] * n,
        out_shape=[inner_shape] * half + [cross_shape] * half,
        scratch_shapes=[
            pltpu.VMEM((3, rows, n * HD), bf16),
            pltpu.SemaphoreType.DMA((3,)),
        ],
        compiler_params=params(56),
        cost_estimate=COST,
    )(place, attn_query, attn_key, attn_value)
    inner, cross = list(packed[:half]), list(packed[half:])

    cols = out_weight.shape[1] // tp
    planes = tp // 2
    y, core = mine // 2, lax.rem(mine, 2)
    swap = [(i, i ^ 1) for i in range(tp)]

    def wanted(plane):
        groups = [2 * plane + 1 - core, 2 * plane + core]
        return jnp.stack([me] + [group * cols for group in groups]).astype(jnp.int32)

    near = [
        fetch(wanted(lax.rem(y + shift, planes)), out_weight, cols) for shift in range(1, planes)
    ]
    for shift in range(1, half):
        inner[shift] = lax.ppermute(inner[shift], "ctx", within(shift))
    cross = [
        lax.ppermute(piece, "ctx", between(shift, 1, 1)) for shift, piece in enumerate(cross)
    ]

    inner[1], *rest = lax.optimization_barrier((inner[1], *inner[2:], near))
    inner[2:], near = rest[:-1], rest[-1]
    back_shape = jax.ShapeDtypeStruct((rows + STAT_ROWS, 2 * HD), bf16)
    over_shape = jax.ShapeDtypeStruct((rows + STAT_ROWS, HD), bf16)
    big, small = pltpu.VMEM((half * rows, 2 * HD), bf16), pltpu.VMEM((half * rows, HD), bf16)
    results = pl.pallas_call(
        functools.partial(inner_kernel, half),
        in_specs=[smem] + [VMEM] * half,
        out_specs=[VMEM] * 2,
        out_shape=[
            jax.ShapeDtypeStruct((half * rows, 2 * HD), f32),
            jax.ShapeDtypeStruct((rows, HD), f32),
        ],
        scratch_shapes=[big] * 3,
        compiler_params=params(24),
        cost_estimate=COST,
    )(place, *inner)
    outs = pl.pallas_call(
        functools.partial(cross_kernel, half),
        in_specs=[smem] + [VMEM] * (n + 2),
        out_specs=[VMEM] * n,
        out_shape=[back_shape] * half + [over_shape] * half,
        scratch_shapes=[small] * 3 + [big, small, pltpu.VMEM((3, n, rows), f32)],
        compiler_params=params(24),
        cost_estimate=COST,
    )(place, *inner, *cross, *results)
    back, over = list(outs[:half]), list(outs[half:])
    for shift in range(1, half):
        back[shift] = lax.ppermute(back[shift], "ctx", within(shift))
    for shift in range(half):
        if shift in T2TIE:
            over[shift], back[1] = lax.optimization_barrier((over[shift], back[1]))
        over[shift] = lax.ppermute(over[shift], "ctx", between(shift, 1, 0))

    tied = (back[1], *over, *back[2:])
    back[1], *tied = lax.optimization_barrier(tied)
    over, back[2:] = tied[:half], tied[half:]
    heads, crossing = None, []
    for shift, (w_give, w_keep) in enumerate(near, 1):
        perm = [(i, (i + 2 * shift) % tp) for i in range(tp)]
        if heads is None:
            heads, give = pl.pallas_call(
                functools.partial(first_kernel, half, 512),
                in_specs=[smem] + [VMEM] * (n + 1),
                out_specs=[VMEM] * 2,
                out_shape=[
                    jax.ShapeDtypeStruct((rows, n * HD), bf16),
                    jax.ShapeDtypeStruct((rows, cols), bf16),
                ],
                compiler_params=params(16),
                cost_estimate=COST,
            )(place, *back, *over, w_give)
        else:
            (give,) = project(heads, [w_give])
        (keep,) = project(heads, [w_keep])
        both = (keep.astype(f32) + lax.ppermute(give, "tp", swap).astype(f32)).astype(bf16)
        crossing.append(lax.ppermute(both, "tp", perm))
        both, heads = lax.optimization_barrier((both, heads))
    out_weight, heads = lax.optimization_barrier((out_weight, heads))
    give, keep = project(heads, fetch(wanted(y), out_weight, cols))
    piece = cols // OWN_PARTS
    swapped = [
        lax.ppermute(give[:, at : at + piece], "tp", swap) for at in range(0, cols, piece)
    ]
    whole = crossing[0]
    if len(crossing) > 1:
        whole = sum(one.astype(f32) for one in crossing)
    return pl.pallas_call(
        last_kernel,
        in_specs=[VMEM] * (2 + OWN_PARTS),
        out_specs=pl.BlockSpec(memory_space=pl.ANY),
        out_shape=jax.ShapeDtypeStruct((rows, cols), bf16),
        scratch_shapes=[
            pltpu.VMEM((rows, cols), bf16),
            pltpu.SemaphoreType.DMA((STEPS,)),
        ],
        compiler_params=params(16),
        cost_estimate=COST,
    )(keep, *swapped, whole)


def solution(mesh):
    def per_device(attn_query, attn_key, attn_value, out_weight):
        heads, n, tp = attn_query.shape[1] // HD, mesh.shape["ctx"], mesh.shape["tp"]
        paired = heads == n and n > 2 and n & (n - 1) == 0 and n <= HD and tp % 2 == 0 and tp > 2
        form = heads_form if paired and attn_query.shape[0] == 2 * HD else gather_form
        return form(attn_query, attn_key, attn_value, out_weight)

    return jax.shard_map(
        per_device,
        mesh=mesh,
        in_specs=(P("ctx", "tp"), P("ctx", "tp"), P("ctx", "tp"), P("tp", None)),
        out_specs=P("ctx", "tp"),
        check_vma=False,
    )
```

```python
import functools

import jax
import jax.numpy as jnp
from jax import lax
from jax.experimental import pallas as pl
from jax.experimental.pallas import tpu as pltpu
from jax.sharding import PartitionSpec as P

HD = 128
MIB = 1 << 20
OWN_PARTS = 2
STEPS = 4
STAT_ROWS = 16
T2TIE = (2, 3)
LOG2E = 1.4426950408889634
FETCH_MIB = 40
COST = pl.CostEstimate(flops=1, bytes_accessed=1, transcendentals=1)
VMEM = pl.BlockSpec(memory_space=pltpu.VMEM)


def params(mib):
    return pltpu.CompilerParams(vmem_limit_bytes=mib * MIB)


def attend(queries, keys, values, query_pos):
    rows = queries.shape[0]
    local_heads = queries.shape[1] // HD
    scale = HD ** (-0.5)
    shaped_q = queries.reshape(rows, local_heads, HD)
    latest = jnp.max(query_pos)
    initial = (
        jnp.full((local_heads, rows), -1e30, jnp.float32),
        jnp.zeros((local_heads, rows), jnp.float32),
        jnp.zeros((local_heads, rows, HD), jnp.float32),
    )
    piece_keys = lax.all_gather(keys, "ctx", axis=0, tiled=True)
    piece_values = lax.all_gather(values, "ctx", axis=0, tiled=True)
    count_rows = piece_keys.shape[0]
    span_rows = 2 * rows

    def one_block(block, state):
        offset = block * span_rows
        block_keys = lax.dynamic_slice_in_dim(piece_keys, offset, span_rows, 0).reshape(
            span_rows, local_heads, HD
        )
        block_values = lax.dynamic_slice_in_dim(piece_values, offset, span_rows, 0).reshape(
            span_rows, local_heads, HD
        )
        key_pos = offset + jnp.arange(span_rows, dtype=jnp.int32)

        def compute(inner):
            maxes, totals, accum = inner
            scores = (
                jnp.einsum("qhd,khd->hqk", shaped_q, block_keys, preferred_element_type=jnp.float32)
                * scale
            )
            allowed = key_pos[None, None, :] <= query_pos[None, :, None]
            new_max = jnp.maximum(maxes, jnp.max(jnp.where(allowed, scores, -1e30), axis=-1))
            factor = jnp.exp(maxes - new_max)
            weights = jnp.where(allowed, jnp.exp(scores - new_max[..., None]), 0.0)
            totals = totals * factor + jnp.sum(weights, axis=-1)
            accum = accum * factor[..., None] + jnp.einsum(
                "hqk,khd->hqd",
                weights.astype(jnp.bfloat16),
                block_values,
                preferred_element_type=jnp.float32,
            )
            return (new_max, totals, accum)

        return lax.cond(jnp.min(key_pos) <= latest, compute, lambda inner: inner, state)

    maxes, totals, accum = lax.fori_loop(0, count_rows // span_rows, one_block, initial)
    result = accum / totals[..., None]
    return jnp.transpose(result, (1, 0, 2)).reshape(rows, local_heads * HD).astype(jnp.bfloat16)


def gather_form(attn_query, attn_key, attn_value, out_weight):
    rows = attn_query.shape[0]
    query_pos = lax.axis_index("ctx") * rows + jnp.arange(rows, dtype=jnp.int32)
    heads = attend(attn_query, attn_key, attn_value, query_pos)
    partial_value = jnp.dot(heads, out_weight, preferred_element_type=jnp.float32)
    return lax.psum_scatter(
        partial_value.astype(jnp.bfloat16), "tp", scatter_dimension=1, tiled=True
    )


def pack_kernel(half, me_ref, q_ref, k_ref, v_ref, *refs):
    inner, cross, (held, sem) = refs[:half], refs[half : 2 * half], refs[2 * half :]
    upper, place = me_ref[0] // half, lax.rem(me_ref[0], half)
    copies = [
        pltpu.make_async_copy(ref, held.at[part], sem.at[part])
        for part, ref in enumerate((q_ref, k_ref, v_ref))
    ]
    for one in copies:
        one.start()
    for part, one in enumerate(copies):
        one.wait()
        for shift in range(half):
            goal = place ^ shift
            cols = pl.ds(pl.multiple_of(goal * 2 * HD, 2 * HD), 2 * HD)
            inner[shift][part] = held[part, :, cols]
    for shift in range(half):
        goal = place ^ shift
        even = pl.ds(pl.multiple_of(goal * 2 * HD, HD), HD)
        odd = pl.ds(pl.multiple_of(goal * 2 * HD + HD, HD), HD)

        @pl.when(upper == 0)
        def _():
            cross[shift][0] = held[1, :, odd]
            cross[shift][1] = held[2, :, odd]

        @pl.when(upper == 1)
        def _():
            cross[shift][0] = held[0, :, even]
            cross[shift][1] = held[0, :, even]


def split3(value):
    high = value.astype(jnp.bfloat16)
    value = value - high.astype(jnp.float32)
    middle = value.astype(jnp.bfloat16)
    return high, middle, (value - middle.astype(jnp.float32)).astype(jnp.bfloat16)


def gather(half, place, rows, pieces, part, out, cols=slice(None)):
    for shift in range(half):
        source = place ^ shift
        at = pl.ds(pl.multiple_of(source * rows, rows), rows)
        piece = pieces[shift][part, :, cols]
        out[at, : piece.shape[1]] = piece


def scores(query, keys):
    dims = (((1,), (1,)), ((), ()))
    return lax.dot_general(query, keys, dims, preferred_element_type=jnp.float32)


def weigh(raw, top, values):
    weights = jnp.exp2((raw - top) * (HD ** (-0.5) * LOG2E))
    acc = jnp.dot(weights.astype(jnp.bfloat16), values, preferred_element_type=jnp.float32)
    return acc[:, HD : HD + 1], acc[:, :HD]


def log_sum(top, total):
    return top * (HD ** (-0.5) * LOG2E) + jnp.log2(total)


def inner_kernel(half, me_ref, *refs):
    inner, (even_ref, odd_ref, table_ref) = refs[:half], refs[half:-3]
    q_all, k_all, v_all = refs[-3:]
    rows = inner[0].shape[1]
    place = lax.rem(me_ref[0], half)
    gather(half, place, rows, inner, 0, q_all)
    gather(half, place, rows, inner, 1, k_all)
    for head in range(2):
        one = v_all.at[head]
        gather(half, place, rows, inner, 2, one, slice(head * HD, (head + 1) * HD))
        one[:, HD:] = jnp.ones((half * rows, HD), jnp.bfloat16)
    diag = lax.broadcasted_iota(jnp.int32, (rows, rows), 1) <= lax.broadcasted_iota(
        jnp.int32, (rows, rows), 0
    )
    lane = lax.broadcasted_iota(jnp.int32, (rows, HD), 1)
    table = jnp.zeros((rows, HD), jnp.float32)
    for block in reversed(range(half)):
        lo, hi = block * rows, (block + 1) * rows
        for head in range(2):
            at = slice(head * HD, (head + 1) * HD)
            query = q_all[lo:hi, at]
            last = jnp.where(diag, scores(query, k_all[lo:hi, at]), -1e30)
            top = jnp.max(last, axis=1, keepdims=True)
            if block:
                early = scores(query, k_all[0:lo, at])
                top = jnp.maximum(top, jnp.max(early, axis=1, keepdims=True))
            total, acc = weigh(last, top, v_all[head, lo:hi, :])
            if block:
                total_early, acc_early = weigh(early, top, v_all[head, 0:lo, :])
                total, acc = total + total_early, acc + acc_early
            if head == 0:
                even_ref[lo:hi, :] = (acc / total).astype(jnp.bfloat16)
            else:
                odd_ref[lo:hi, :] = acc / total
            table = jnp.where(lane == head * half + block, log_sum(top, total), table)
    table_ref[...] = table


def cross_kernel(half, me_ref, *refs):
    inner, cross, refs = refs[:half], refs[half : 2 * half], refs[2 * half :]
    (even_ref, odd_ref, table_ref), refs = refs[:3], refs[3:]
    back, over = refs[:half], refs[half : 2 * half]
    q_x, k_x, v_x, o_odd, o_x, stats = refs[2 * half :]
    rows = inner[0].shape[1]
    upper, place = me_ref[0] // half, lax.rem(me_ref[0], half)

    @pl.when(upper == 0)
    def _():
        gather(half, place, rows, cross, 0, q_x)
        gather(half, place, rows, inner, 1, k_x, slice(0, HD))
        gather(half, place, rows, inner, 2, v_x, slice(0, HD))

    @pl.when(upper == 1)
    def _():
        gather(half, place, rows, inner, 0, q_x, slice(HD, 2 * HD))
        gather(half, place, rows, cross, 0, k_x)
        gather(half, place, rows, cross, 1, v_x)

    v_x[:, HD:] = jnp.ones((half * rows, HD), jnp.bfloat16)
    lane = lax.broadcasted_iota(jnp.int32, (rows, HD), 1)
    logs = table_ref[...]
    table = logs
    for block in range(half):
        lo, hi = block * rows, (block + 1) * rows
        raw = scores(q_x[lo:hi, :], k_x[...])
        top = jnp.max(raw, axis=1, keepdims=True)
        total, acc = weigh(raw, top, v_x[...])
        result = acc / total
        o_x[lo:hi, :] = result.astype(jnp.bfloat16)
        log_x = log_sum(top, total)
        table = jnp.where(lane == half + block, log_x, table)
        gap = jnp.where(upper == 1, log_x - logs[:, half + block : half + block + 1], -1e30)
        near, far = 1.0 / (1.0 + jnp.exp2(gap)), 1.0 / (1.0 + jnp.exp2(-gap))
        o_odd[lo:hi, :] = (near * odd_ref[lo:hi, :] + far * result).astype(jnp.bfloat16)
    turned = jnp.transpose(table)
    for i, part in enumerate(split3(turned[0 : 2 * half, :])):
        stats[i] = part.astype(jnp.float32)
    for shift in range(half):
        goal = place ^ shift
        at = pl.ds(pl.multiple_of(goal * rows, rows), rows)
        back[shift][0:rows, :HD] = even_ref[at, :]
        back[shift][0:rows, HD:] = o_odd[at, :]
        over[shift][0:rows, :] = o_x[at, :]
        for out, first in ((back[shift], 0), (over[shift], half)):
            wide = out.shape[1]
            lines = [stats[i, pl.ds(first + goal, 1), :] for i in range(3)]
            lines = [line[:, at : at + wide] for line in lines for at in range(0, rows, wide)]
            empty = jnp.zeros((STAT_ROWS - len(lines), wide), jnp.float32)
            out[rows:, :] = jnp.concatenate(lines + [empty], axis=0).astype(jnp.bfloat16)


def assemble(half, me_ref, back, over, heads):
    rows = heads.shape[0]
    upper, place = me_ref[0] // half, lax.rem(me_ref[0], half)

    def read_log(piece):
        steps = rows // piece.shape[1]
        block = piece[rows:, :].astype(jnp.float32)
        sums = [
            block[i : i + 1, :] + block[steps + i : steps + i + 1, :]
            + block[2 * steps + i : 2 * steps + i + 1, :]
            for i in range(steps)
        ]
        return jnp.concatenate(sums, axis=1)

    gaps = []
    for shift in range(half):
        gap = read_log(over[shift]) - read_log(back[shift])
        gaps.append(jnp.where(upper == 1, gap, -1e30))
    table = jnp.concatenate(gaps + [jnp.zeros((HD - half, rows), jnp.float32)], axis=0)
    table = jnp.transpose(table)
    for shift in range(half):
        source = place ^ shift
        even = pl.ds(pl.multiple_of(source * 2 * HD, HD), HD)
        odd = pl.ds(pl.multiple_of(source * 2 * HD + HD, HD), HD)
        gap = table[:, shift : shift + 1]
        near = 1.0 / (1.0 + jnp.exp2(gap))
        far = 1.0 / (1.0 + jnp.exp2(-gap))
        merged = near * back[shift][0:rows, 0:HD].astype(jnp.float32)
        merged += far * over[shift][0:rows, :].astype(jnp.float32)
        heads[:, even] = merged.astype(jnp.bfloat16)
        heads[:, odd] = back[shift][0:rows, HD:]


def multiply(heads, weight, out, tile):
    for at in range(0, out.shape[1], tile):
        out[:, at : at + tile] = jnp.dot(
            heads[...], weight[:, at : at + tile], preferred_element_type=jnp.float32
        ).astype(jnp.bfloat16)


def first_kernel(half, tile, me_ref, *refs):
    back, over, (weight, heads, out) = refs[:half], refs[half : 2 * half], refs[2 * half :]
    assemble(half, me_ref, back, over, heads)
    multiply(heads, weight, out, tile)


def later_kernel(tile, heads, *refs):
    count = len(refs) // 2
    for weight, out in zip(refs[:count], refs[count:]):
        multiply(heads, weight, out, tile)


def last_kernel(keep, *refs):
    swapped, (whole, out, held, sem) = refs[:OWN_PARTS], refs[OWN_PARTS:]
    rows, cols = keep.shape
    step, wide = rows // STEPS, cols // OWN_PARTS
    copies = []
    for i in range(STEPS):
        at = slice(i * step, (i + 1) * step)
        for j, part in enumerate(swapped):
            here = slice(j * wide, (j + 1) * wide)
            total = keep[at, here].astype(jnp.float32) + part[at, :].astype(jnp.float32)
            held[at, here] = (total + whole[at, here].astype(jnp.float32)).astype(jnp.bfloat16)
        rows_at = pl.ds(i * step, step)
        copies.append(pltpu.make_async_copy(held.at[rows_at], out.at[rows_at], sem.at[i]))
        copies[-1].start()
    for one in copies:
        one.wait()


def project(heads, weights):
    out = jax.ShapeDtypeStruct((heads.shape[0], weights[0].shape[1]), jnp.bfloat16)
    return pl.pallas_call(
        functools.partial(later_kernel, 512),
        in_specs=[VMEM] * (1 + len(weights)),
        out_specs=[VMEM] * len(weights),
        out_shape=[out] * len(weights),
        compiler_params=params(16),
        cost_estimate=COST,
    )(heads, *weights)


def fetch_kernel(place_ref, w_ref, *refs):
    outs, sem = refs[:-1], refs[-1]
    cols = outs[0].shape[1]
    copies = []
    for which, out in enumerate(outs):
        at = pl.ds(pl.multiple_of(place_ref[1 + which], cols), cols)
        copies.append(pltpu.make_async_copy(w_ref.at[:, at], out, sem.at[which]))
    for one in copies:
        one.start()
    for one in copies:
        one.wait()


def fetch(place, weight, cols):
    depth, groups = weight.shape[0], place.shape[0] - 1
    return pl.pallas_call(
        fetch_kernel,
        in_specs=[pl.BlockSpec(memory_space=pltpu.SMEM), pl.BlockSpec(memory_space=pl.ANY)],
        out_specs=[VMEM] * groups,
        out_shape=[jax.ShapeDtypeStruct((depth, cols), weight.dtype)] * groups,
        scratch_shapes=[pltpu.SemaphoreType.DMA((groups,))],
        compiler_params=params(FETCH_MIB),
        cost_estimate=pl.CostEstimate(
            flops=1, bytes_accessed=4 * depth * cols * groups, transcendentals=1
        ),
    )(place, weight)


def heads_form(attn_query, attn_key, attn_value, out_weight):
    n, tp = lax.axis_size("ctx"), lax.axis_size("tp")
    half = n // 2
    rows = attn_query.shape[0]
    bf16, f32 = jnp.bfloat16, jnp.float32
    me, mine = lax.axis_index("ctx"), lax.axis_index("tp")
    place = me.astype(jnp.int32).reshape(1)
    smem = pl.BlockSpec(memory_space=pltpu.SMEM)

    def within(shift):
        return [(i, i ^ shift) for i in range(n)]

    def between(shift, lower, upper):
        up = [(i, half + (i ^ shift)) for i in range(half)]
        down = [(half + i, i ^ shift) for i in range(half)]
        return up * lower + down * upper

    inner_shape = jax.ShapeDtypeStruct((3, rows, 2 * HD), bf16)
    cross_shape = jax.ShapeDtypeStruct((2, rows, HD), bf16)
    packed = pl.pallas_call(
        functools.partial(pack_kernel, half),
        in_specs=[smem] + [pl.BlockSpec(memory_space=pl.ANY)] * 3,
        out_specs=[VMEM] * n,
        out_shape=[inner_shape] * half + [cross_shape] * half,
        scratch_shapes=[
            pltpu.VMEM((3, rows, n * HD), bf16),
            pltpu.SemaphoreType.DMA((3,)),
        ],
        compiler_params=params(56),
        cost_estimate=COST,
    )(place, attn_query, attn_key, attn_value)
    inner, cross = list(packed[:half]), list(packed[half:])

    cols = out_weight.shape[1] // tp
    planes = tp // 2
    y, core = mine // 2, lax.rem(mine, 2)
    swap = [(i, i ^ 1) for i in range(tp)]

    def wanted(plane):
        groups = [2 * plane + 1 - core, 2 * plane + core]
        return jnp.stack([me] + [group * cols for group in groups]).astype(jnp.int32)

    near = [
        fetch(wanted(lax.rem(y + shift, planes)), out_weight, cols) for shift in range(1, planes)
    ]
    for shift in range(1, half):
        inner[shift] = lax.ppermute(inner[shift], "ctx", within(shift))
    cross = [
        lax.ppermute(piece, "ctx", between(shift, 1, 1)) for shift, piece in enumerate(cross)
    ]

    inner[1], *rest = lax.optimization_barrier((inner[1], *inner[2:], near))
    inner[2:], near = rest[:-1], rest[-1]
    back_shape = jax.ShapeDtypeStruct((rows + STAT_ROWS, 2 * HD), bf16)
    over_shape = jax.ShapeDtypeStruct((rows + STAT_ROWS, HD), bf16)
    big, small = pltpu.VMEM((half * rows, 2 * HD), bf16), pltpu.VMEM((half * rows, HD), bf16)
    results = pl.pallas_call(
        functools.partial(inner_kernel, half),
        in_specs=[smem] + [VMEM] * half,
        out_specs=[VMEM] * 3,
        out_shape=[
            jax.ShapeDtypeStruct((half * rows, HD), bf16),
            jax.ShapeDtypeStruct((half * rows, HD), f32),
            jax.ShapeDtypeStruct((rows, HD), f32),
        ],
        scratch_shapes=[big] * 2 + [pltpu.VMEM((2, half * rows, 2 * HD), bf16)],
        compiler_params=params(24),
        cost_estimate=COST,
    )(place, *inner)
    outs = pl.pallas_call(
        functools.partial(cross_kernel, half),
        in_specs=[smem] + [VMEM] * (n + 3),
        out_specs=[VMEM] * n,
        out_shape=[back_shape] * half + [over_shape] * half,
        scratch_shapes=[small] * 2 + [big] + [small] * 2 + [ pltpu.VMEM((3, n, rows), f32)],
        compiler_params=params(24),
        cost_estimate=COST,
    )(place, *inner, *cross, *results)
    back, over = list(outs[:half]), list(outs[half:])
    for shift in range(1, half):
        back[shift] = lax.ppermute(back[shift], "ctx", within(shift))
    for shift in range(half):
        if shift in T2TIE:
            over[shift], back[1] = lax.optimization_barrier((over[shift], back[1]))
        over[shift] = lax.ppermute(over[shift], "ctx", between(shift, 1, 0))

    tied = (back[1], *over, *back[2:])
    back[1], *tied = lax.optimization_barrier(tied)
    over, back[2:] = tied[:half], tied[half:]
    heads, crossing = None, []
    for shift, (w_give, w_keep) in enumerate(near, 1):
        perm = [(i, (i + 2 * shift) % tp) for i in range(tp)]
        if heads is None:
            heads, give = pl.pallas_call(
                functools.partial(first_kernel, half, 512),
                in_specs=[smem] + [VMEM] * (n + 1),
                out_specs=[VMEM] * 2,
                out_shape=[
                    jax.ShapeDtypeStruct((rows, n * HD), bf16),
                    jax.ShapeDtypeStruct((rows, cols), bf16),
                ],
                compiler_params=params(16),
                cost_estimate=COST,
            )(place, *back, *over, w_give)
        else:
            (give,) = project(heads, [w_give])
        (keep,) = project(heads, [w_keep])
        both = (keep.astype(f32) + lax.ppermute(give, "tp", swap).astype(f32)).astype(bf16)
        crossing.append(lax.ppermute(both, "tp", perm))
        both, heads = lax.optimization_barrier((both, heads))
    out_weight, heads = lax.optimization_barrier((out_weight, heads))
    give, keep = project(heads, fetch(wanted(y), out_weight, cols))
    piece = cols // OWN_PARTS
    swapped = [
        lax.ppermute(give[:, at : at + piece], "tp", swap) for at in range(0, cols, piece)
    ]
    whole = crossing[0]
    if len(crossing) > 1:
        whole = sum(one.astype(f32) for one in crossing)
    return pl.pallas_call(
        last_kernel,
        in_specs=[VMEM] * (2 + OWN_PARTS),
        out_specs=pl.BlockSpec(memory_space=pl.ANY),
        out_shape=jax.ShapeDtypeStruct((rows, cols), bf16),
        scratch_shapes=[
            pltpu.VMEM((rows, cols), bf16),
            pltpu.SemaphoreType.DMA((STEPS,)),
        ],
        compiler_params=params(16),
        cost_estimate=COST,
    )(keep, *swapped, whole)


def solution(mesh):
    def per_device(attn_query, attn_key, attn_value, out_weight):
        heads, n, tp = attn_query.shape[1] // HD, mesh.shape["ctx"], mesh.shape["tp"]
        paired = heads == n and n > 2 and n & (n - 1) == 0 and n <= HD and tp % 2 == 0 and tp > 2
        form = heads_form if paired and attn_query.shape[0] == 2 * HD else gather_form
        return form(attn_query, attn_key, attn_value, out_weight)

    return jax.shard_map(
        per_device,
        mesh=mesh,
        in_specs=(P("ctx", "tp"), P("ctx", "tp"), P("ctx", "tp"), P("tp", None)),
        out_specs=P("ctx", "tp"),
        check_vma=False,
    )
```

```python
import functools

import jax
import jax.numpy as jnp
from jax import lax
from jax.experimental import pallas as pl
from jax.experimental.pallas import tpu as pltpu
from jax.sharding import PartitionSpec as P

HD = 128
MIB = 1 << 20
OWN_PARTS = 2
STEPS = 8
STAT_ROWS = 16
T2TIE = (2, 3)
LOG2E = 1.4426950408889634
FETCH_MIB = 40
COST = pl.CostEstimate(flops=1, bytes_accessed=1, transcendentals=1)
VMEM = pl.BlockSpec(memory_space=pltpu.VMEM)


def params(mib):
    return pltpu.CompilerParams(vmem_limit_bytes=mib * MIB)


def attend(queries, keys, values, query_pos):
    rows = queries.shape[0]
    local_heads = queries.shape[1] // HD
    scale = HD ** (-0.5)
    shaped_q = queries.reshape(rows, local_heads, HD)
    latest = jnp.max(query_pos)
    initial = (
        jnp.full((local_heads, rows), -1e30, jnp.float32),
        jnp.zeros((local_heads, rows), jnp.float32),
        jnp.zeros((local_heads, rows, HD), jnp.float32),
    )
    piece_keys = lax.all_gather(keys, "ctx", axis=0, tiled=True)
    piece_values = lax.all_gather(values, "ctx", axis=0, tiled=True)
    count_rows = piece_keys.shape[0]
    span_rows = 2 * rows

    def one_block(block, state):
        offset = block * span_rows
        block_keys = lax.dynamic_slice_in_dim(piece_keys, offset, span_rows, 0).reshape(
            span_rows, local_heads, HD
        )
        block_values = lax.dynamic_slice_in_dim(piece_values, offset, span_rows, 0).reshape(
            span_rows, local_heads, HD
        )
        key_pos = offset + jnp.arange(span_rows, dtype=jnp.int32)

        def compute(inner):
            maxes, totals, accum = inner
            scores = (
                jnp.einsum("qhd,khd->hqk", shaped_q, block_keys, preferred_element_type=jnp.float32)
                * scale
            )
            allowed = key_pos[None, None, :] <= query_pos[None, :, None]
            new_max = jnp.maximum(maxes, jnp.max(jnp.where(allowed, scores, -1e30), axis=-1))
            factor = jnp.exp(maxes - new_max)
            weights = jnp.where(allowed, jnp.exp(scores - new_max[..., None]), 0.0)
            totals = totals * factor + jnp.sum(weights, axis=-1)
            accum = accum * factor[..., None] + jnp.einsum(
                "hqk,khd->hqd",
                weights.astype(jnp.bfloat16),
                block_values,
                preferred_element_type=jnp.float32,
            )
            return (new_max, totals, accum)

        return lax.cond(jnp.min(key_pos) <= latest, compute, lambda inner: inner, state)

    maxes, totals, accum = lax.fori_loop(0, count_rows // span_rows, one_block, initial)
    result = accum / totals[..., None]
    return jnp.transpose(result, (1, 0, 2)).reshape(rows, local_heads * HD).astype(jnp.bfloat16)


def gather_form(attn_query, attn_key, attn_value, out_weight):
    rows = attn_query.shape[0]
    query_pos = lax.axis_index("ctx") * rows + jnp.arange(rows, dtype=jnp.int32)
    heads = attend(attn_query, attn_key, attn_value, query_pos)
    partial_value = jnp.dot(heads, out_weight, preferred_element_type=jnp.float32)
    return lax.psum_scatter(
        partial_value.astype(jnp.bfloat16), "tp", scatter_dimension=1, tiled=True
    )


def pack_kernel(half, me_ref, q_ref, k_ref, v_ref, *refs):
    inner, cross, (held, sem) = refs[:half], refs[half : 2 * half], refs[2 * half :]
    upper, place = me_ref[0] // half, lax.rem(me_ref[0], half)
    copies = [
        pltpu.make_async_copy(ref, held.at[part], sem.at[part])
        for part, ref in enumerate((q_ref, k_ref, v_ref))
    ]
    for one in copies:
        one.start()
    for part, one in enumerate(copies):
        one.wait()
        for shift in range(half):
            goal = place ^ shift
            cols = pl.ds(pl.multiple_of(goal * 2 * HD, 2 * HD), 2 * HD)
            inner[shift][part] = held[part, :, cols]
    for shift in range(half):
        goal = place ^ shift
        even = pl.ds(pl.multiple_of(goal * 2 * HD, HD), HD)
        odd = pl.ds(pl.multiple_of(goal * 2 * HD + HD, HD), HD)

        @pl.when(upper == 0)
        def _():
            cross[shift][0] = held[1, :, odd]
            cross[shift][1] = held[2, :, odd]

        @pl.when(upper == 1)
        def _():
            cross[shift][0] = held[0, :, even]
            cross[shift][1] = held[0, :, even]


def split3(value):
    high = value.astype(jnp.bfloat16)
    value = value - high.astype(jnp.float32)
    middle = value.astype(jnp.bfloat16)
    return high, middle, (value - middle.astype(jnp.float32)).astype(jnp.bfloat16)


def gather(half, place, rows, pieces, part, out, cols=slice(None)):
    for shift in range(half):
        source = place ^ shift
        at = pl.ds(pl.multiple_of(source * rows, rows), rows)
        piece = pieces[shift][part, :, cols]
        out[at, : piece.shape[1]] = piece


def scores(query, keys):
    dims = (((1,), (1,)), ((), ()))
    return lax.dot_general(query, keys, dims, preferred_element_type=jnp.float32)


def weigh(raw, top, values):
    weights = jnp.exp2((raw - top) * (HD ** (-0.5) * LOG2E))
    acc = jnp.dot(weights.astype(jnp.bfloat16), values, preferred_element_type=jnp.float32)
    return acc[:, HD : HD + 1], acc[:, :HD]


def log_sum(top, total):
    return top * (HD ** (-0.5) * LOG2E) + jnp.log2(total)


def inner_kernel(half, me_ref, *refs):
    inner, (even_ref, odd_ref, table_ref) = refs[:half], refs[half:-3]
    q_all, k_all, v_all = refs[-3:]
    rows = inner[0].shape[1]
    place = lax.rem(me_ref[0], half)
    gather(half, place, rows, inner, 0, q_all)
    gather(half, place, rows, inner, 1, k_all)
    for head in range(2):
        one = v_all.at[head]
        gather(half, place, rows, inner, 2, one, slice(head * HD, (head + 1) * HD))
        one[:, HD:] = jnp.ones((half * rows, HD), jnp.bfloat16)
    diag = lax.broadcasted_iota(jnp.int32, (rows, rows), 1) <= lax.broadcasted_iota(
        jnp.int32, (rows, rows), 0
    )
    lane = lax.broadcasted_iota(jnp.int32, (rows, HD), 1)
    table = jnp.zeros((rows, HD), jnp.float32)
    for block in reversed(range(half)):
        lo, hi = block * rows, (block + 1) * rows
        for head in range(2):
            at = slice(head * HD, (head + 1) * HD)
            query = q_all[lo:hi, at]
            last = jnp.where(diag, scores(query, k_all[lo:hi, at]), -1e30)
            top = jnp.max(last, axis=1, keepdims=True)
            if block:
                early = scores(query, k_all[0:lo, at])
                top = jnp.maximum(top, jnp.max(early, axis=1, keepdims=True))
            total, acc = weigh(last, top, v_all[head, lo:hi, :])
            if block:
                total_early, acc_early = weigh(early, top, v_all[head, 0:lo, :])
                total, acc = total + total_early, acc + acc_early
            if head == 0:
                even_ref[lo:hi, :] = (acc / total).astype(jnp.bfloat16)
            else:
                odd_ref[lo:hi, :] = acc / total
            table = jnp.where(lane == head * half + block, log_sum(top, total), table)
    table_ref[...] = table


def cross_kernel(half, me_ref, *refs):
    inner, cross, refs = refs[:half], refs[half : 2 * half], refs[2 * half :]
    (even_ref, odd_ref, table_ref), refs = refs[:3], refs[3:]
    back, over = refs[:half], refs[half : 2 * half]
    q_x, k_x, v_x, o_odd, o_x, stats = refs[2 * half :]
    rows = inner[0].shape[1]
    upper, place = me_ref[0] // half, lax.rem(me_ref[0], half)

    @pl.when(upper == 0)
    def _():
        gather(half, place, rows, cross, 0, q_x)
        gather(half, place, rows, inner, 1, k_x, slice(0, HD))
        gather(half, place, rows, inner, 2, v_x, slice(0, HD))

    @pl.when(upper == 1)
    def _():
        gather(half, place, rows, inner, 0, q_x, slice(HD, 2 * HD))
        gather(half, place, rows, cross, 0, k_x)
        gather(half, place, rows, cross, 1, v_x)

    v_x[:, HD:] = jnp.ones((half * rows, HD), jnp.bfloat16)
    lane = lax.broadcasted_iota(jnp.int32, (rows, HD), 1)
    logs = table_ref[...]
    table = logs
    for block in range(half):
        lo, hi = block * rows, (block + 1) * rows
        raw = scores(q_x[lo:hi, :], k_x[...])
        top = jnp.max(raw, axis=1, keepdims=True)
        total, acc = weigh(raw, top, v_x[...])
        result = acc / total
        o_x[lo:hi, :] = result.astype(jnp.bfloat16)
        log_x = log_sum(top, total)
        table = jnp.where(lane == half + block, log_x, table)
        gap = jnp.where(upper == 1, log_x - logs[:, half + block : half + block + 1], -1e30)
        near, far = 1.0 / (1.0 + jnp.exp2(gap)), 1.0 / (1.0 + jnp.exp2(-gap))
        o_odd[lo:hi, :] = (near * odd_ref[lo:hi, :] + far * result).astype(jnp.bfloat16)
    turned = jnp.transpose(table)
    for i, part in enumerate(split3(turned[0 : 2 * half, :])):
        stats[i] = part.astype(jnp.float32)
    for shift in range(half):
        goal = place ^ shift
        at = pl.ds(pl.multiple_of(goal * rows, rows), rows)
        back[shift][0:rows, :HD] = even_ref[at, :]
        back[shift][0:rows, HD:] = o_odd[at, :]
        over[shift][0:rows, :] = o_x[at, :]
        for out, first in ((back[shift], 0), (over[shift], half)):
            wide = out.shape[1]
            lines = [stats[i, pl.ds(first + goal, 1), :] for i in range(3)]
            lines = [line[:, at : at + wide] for line in lines for at in range(0, rows, wide)]
            empty = jnp.zeros((STAT_ROWS - len(lines), wide), jnp.float32)
            out[rows:, :] = jnp.concatenate(lines + [empty], axis=0).astype(jnp.bfloat16)


def assemble(half, me_ref, back, over, heads):
    rows = heads.shape[0]
    upper, place = me_ref[0] // half, lax.rem(me_ref[0], half)

    def read_log(piece):
        steps = rows // piece.shape[1]
        block = piece[rows:, :].astype(jnp.float32)
        sums = [
            block[i : i + 1, :] + block[steps + i : steps + i + 1, :]
            + block[2 * steps + i : 2 * steps + i + 1, :]
            for i in range(steps)
        ]
        return jnp.concatenate(sums, axis=1)

    @pl.when(upper == 0)
    def _():
        for shift in range(half):
            wide = pl.ds(pl.multiple_of((place ^ shift) * 2 * HD, 2 * HD), 2 * HD)
            heads[:, wide] = back[shift][0:rows, :]

    @pl.when(upper == 1)
    def _():
        gaps = [read_log(over[shift]) - read_log(back[shift]) for shift in range(half)]
        table = jnp.concatenate(gaps + [jnp.zeros((HD - half, rows), jnp.float32)], axis=0)
        table = jnp.transpose(table)
        for shift in range(half):
            even = pl.ds(pl.multiple_of((place ^ shift) * 2 * HD, HD), HD)
            odd = pl.ds(pl.multiple_of((place ^ shift) * 2 * HD + HD, HD), HD)
            gap = table[:, shift : shift + 1]
            near = 1.0 / (1.0 + jnp.exp2(gap))
            far = 1.0 / (1.0 + jnp.exp2(-gap))
            merged = near * back[shift][0:rows, 0:HD].astype(jnp.float32)
            merged += far * over[shift][0:rows, :].astype(jnp.float32)
            heads[:, even] = merged.astype(jnp.bfloat16)
            heads[:, odd] = back[shift][0:rows, HD:]


def multiply(heads, weight, out, tile):
    for at in range(0, out.shape[1], tile):
        out[:, at : at + tile] = jnp.dot(
            heads[...], weight[:, at : at + tile], preferred_element_type=jnp.float32
        ).astype(jnp.bfloat16)


def first_kernel(half, tile, me_ref, *refs):
    back, over, (weight, heads, out) = refs[:half], refs[half : 2 * half], refs[2 * half :]
    assemble(half, me_ref, back, over, heads)
    multiply(heads, weight, out, tile)


def later_kernel(tile, heads, *refs):
    count = len(refs) // 2
    for weight, out in zip(refs[:count], refs[count:]):
        multiply(heads, weight, out, tile)


def last_kernel(keep, *refs):
    swapped, (whole, out, held, sem) = refs[:OWN_PARTS], refs[OWN_PARTS:]
    rows, cols = keep.shape
    step, wide = rows // STEPS, cols // OWN_PARTS
    copies = []
    for i in range(STEPS):
        at = slice(i * step, (i + 1) * step)
        for j, part in enumerate(swapped):
            here = slice(j * wide, (j + 1) * wide)
            total = keep[at, here].astype(jnp.float32) + part[at, :].astype(jnp.float32)
            held[at, here] = (total + whole[at, here].astype(jnp.float32)).astype(jnp.bfloat16)
        rows_at = pl.ds(i * step, step)
        copies.append(pltpu.make_async_copy(held.at[rows_at], out.at[rows_at], sem.at[i]))
        copies[-1].start()
    for one in copies:
        one.wait()


def project(heads, weights):
    out = jax.ShapeDtypeStruct((heads.shape[0], weights[0].shape[1]), jnp.bfloat16)
    return pl.pallas_call(
        functools.partial(later_kernel, weights[0].shape[1]),
        in_specs=[VMEM] * (1 + len(weights)),
        out_specs=[VMEM] * len(weights),
        out_shape=[out] * len(weights),
        compiler_params=params(16),
        cost_estimate=COST,
    )(heads, *weights)


def fetch_kernel(place_ref, w_ref, *refs):
    outs, sem = refs[:-1], refs[-1]
    cols = outs[0].shape[1]
    copies = []
    for which, out in enumerate(outs):
        at = pl.ds(pl.multiple_of(place_ref[1 + which], cols), cols)
        copies.append(pltpu.make_async_copy(w_ref.at[:, at], out, sem.at[which]))
    for one in copies:
        one.start()
    for one in copies:
        one.wait()


def fetch(place, weight, cols):
    depth, groups = weight.shape[0], place.shape[0] - 1
    return pl.pallas_call(
        fetch_kernel,
        in_specs=[pl.BlockSpec(memory_space=pltpu.SMEM), pl.BlockSpec(memory_space=pl.ANY)],
        out_specs=[VMEM] * groups,
        out_shape=[jax.ShapeDtypeStruct((depth, cols), weight.dtype)] * groups,
        scratch_shapes=[pltpu.SemaphoreType.DMA((groups,))],
        compiler_params=params(FETCH_MIB),
        cost_estimate=pl.CostEstimate(
            flops=1, bytes_accessed=4 * depth * cols * groups, transcendentals=1
        ),
    )(place, weight)


def heads_form(attn_query, attn_key, attn_value, out_weight):
    n, tp = lax.axis_size("ctx"), lax.axis_size("tp")
    half = n // 2
    rows = attn_query.shape[0]
    bf16, f32 = jnp.bfloat16, jnp.float32
    me, mine = lax.axis_index("ctx"), lax.axis_index("tp")
    place = me.astype(jnp.int32).reshape(1)
    smem = pl.BlockSpec(memory_space=pltpu.SMEM)

    def within(shift):
        return [(i, i ^ shift) for i in range(n)]

    def between(shift, lower, upper):
        up = [(i, half + (i ^ shift)) for i in range(half)]
        down = [(half + i, i ^ shift) for i in range(half)]
        return up * lower + down * upper

    inner_shape = jax.ShapeDtypeStruct((3, rows, 2 * HD), bf16)
    cross_shape = jax.ShapeDtypeStruct((2, rows, HD), bf16)
    packed = pl.pallas_call(
        functools.partial(pack_kernel, half),
        in_specs=[smem] + [pl.BlockSpec(memory_space=pl.ANY)] * 3,
        out_specs=[VMEM] * n,
        out_shape=[inner_shape] * half + [cross_shape] * half,
        scratch_shapes=[
            pltpu.VMEM((3, rows, n * HD), bf16),
            pltpu.SemaphoreType.DMA((3,)),
        ],
        compiler_params=params(56),
        cost_estimate=COST,
    )(place, attn_query, attn_key, attn_value)
    inner, cross = list(packed[:half]), list(packed[half:])

    cols = out_weight.shape[1] // tp
    planes = tp // 2
    y, core = mine // 2, lax.rem(mine, 2)
    swap = [(i, i ^ 1) for i in range(tp)]

    def wanted(plane):
        groups = [2 * plane + 1 - core, 2 * plane + core]
        return jnp.stack([me] + [group * cols for group in groups]).astype(jnp.int32)

    near = [
        fetch(wanted(lax.rem(y + shift, planes)), out_weight, cols) for shift in range(1, planes)
    ]
    for shift in range(1, half):
        inner[shift] = lax.ppermute(inner[shift], "ctx", within(shift))
    cross = [
        lax.ppermute(piece, "ctx", between(shift, 1, 1)) for shift, piece in enumerate(cross)
    ]

    inner[1], *rest = lax.optimization_barrier((inner[1], *inner[2:], near))
    inner[2:], near = rest[:-1], rest[-1]
    back_shape = jax.ShapeDtypeStruct((rows + STAT_ROWS, 2 * HD), bf16)
    over_shape = jax.ShapeDtypeStruct((rows + STAT_ROWS, HD), bf16)
    big, small = pltpu.VMEM((half * rows, 2 * HD), bf16), pltpu.VMEM((half * rows, HD), bf16)
    results = pl.pallas_call(
        functools.partial(inner_kernel, half),
        in_specs=[smem] + [VMEM] * half,
        out_specs=[VMEM] * 3,
        out_shape=[
            jax.ShapeDtypeStruct((half * rows, HD), bf16),
            jax.ShapeDtypeStruct((half * rows, HD), f32),
            jax.ShapeDtypeStruct((rows, HD), f32),
        ],
        scratch_shapes=[big] * 2 + [pltpu.VMEM((2, half * rows, 2 * HD), bf16)],
        compiler_params=params(24),
        cost_estimate=COST,
    )(place, *inner)
    outs = pl.pallas_call(
        functools.partial(cross_kernel, half),
        in_specs=[smem] + [VMEM] * (n + 3),
        out_specs=[VMEM] * n,
        out_shape=[back_shape] * half + [over_shape] * half,
        scratch_shapes=[small] * 2 + [big] + [small] * 2 + [ pltpu.VMEM((3, n, rows), f32)],
        compiler_params=params(24),
        cost_estimate=COST,
    )(place, *inner, *cross, *results)
    back, over = list(outs[:half]), list(outs[half:])
    for shift in range(1, half):
        back[shift] = lax.ppermute(back[shift], "ctx", within(shift))
    for shift in range(half):
        if shift in T2TIE:
            over[shift], back[1] = lax.optimization_barrier((over[shift], back[1]))
        over[shift] = lax.ppermute(over[shift], "ctx", between(shift, 1, 0))

    tied = (back[1], *over, *back[2:])
    back[1], *tied = lax.optimization_barrier(tied)
    over, back[2:] = tied[:half], tied[half:]
    heads, crossing = None, []
    for shift, (w_give, w_keep) in enumerate(near, 1):
        perm = [(i, (i + 2 * shift) % tp) for i in range(tp)]
        if heads is None:
            heads, give = pl.pallas_call(
                functools.partial(first_kernel, half, cols),
                in_specs=[smem] + [VMEM] * (n + 1),
                out_specs=[VMEM] * 2,
                out_shape=[
                    jax.ShapeDtypeStruct((rows, n * HD), bf16),
                    jax.ShapeDtypeStruct((rows, cols), bf16),
                ],
                compiler_params=params(16),
                cost_estimate=COST,
            )(place, *back, *over, w_give)
        else:
            (give,) = project(heads, [w_give])
        (keep,) = project(heads, [w_keep])
        both = (keep.astype(f32) + lax.ppermute(give, "tp", swap).astype(f32)).astype(bf16)
        crossing.append(lax.ppermute(both, "tp", perm))
        both, heads = lax.optimization_barrier((both, heads))
    out_weight, heads = lax.optimization_barrier((out_weight, heads))
    give, keep = project(heads, fetch(wanted(y), out_weight, cols))
    piece = cols // OWN_PARTS
    swapped = [
        lax.ppermute(give[:, at : at + piece], "tp", swap) for at in range(0, cols, piece)
    ]
    whole = crossing[0]
    if len(crossing) > 1:
        whole = sum(one.astype(f32) for one in crossing)
    return pl.pallas_call(
        last_kernel,
        in_specs=[VMEM] * (2 + OWN_PARTS),
        out_specs=pl.BlockSpec(memory_space=pl.ANY),
        out_shape=jax.ShapeDtypeStruct((rows, cols), bf16),
        scratch_shapes=[
            pltpu.VMEM((rows, cols), bf16),
            pltpu.SemaphoreType.DMA((STEPS,)),
        ],
        compiler_params=params(16),
        cost_estimate=COST,
    )(keep, *swapped, whole)


def solution(mesh):
    def per_device(attn_query, attn_key, attn_value, out_weight):
        heads, n, tp = attn_query.shape[1] // HD, mesh.shape["ctx"], mesh.shape["tp"]
        paired = heads == n and n > 2 and n & (n - 1) == 0 and n <= HD and tp % 2 == 0 and tp > 2
        form = heads_form if paired and attn_query.shape[0] == 2 * HD else gather_form
        return form(attn_query, attn_key, attn_value, out_weight)

    return jax.shard_map(
        per_device,
        mesh=mesh,
        in_specs=(P("ctx", "tp"), P("ctx", "tp"), P("ctx", "tp"), P("tp", None)),
        out_specs=P("ctx", "tp"),
        check_vma=False,
    )
```

```python
import functools

import jax
import jax.numpy as jnp
from jax import lax
from jax.experimental import pallas as pl
from jax.experimental.pallas import tpu as pltpu
from jax.sharding import PartitionSpec as P

HD = 128
MIB = 1 << 20
OWN_PARTS = 2
STEPS = 4
STAT_ROWS = 16
T2TIE = (2, 3)
LOG2E = 1.4426950408889634
FETCH_MIB = 40
COST = pl.CostEstimate(flops=1, bytes_accessed=1, transcendentals=1)
VMEM = pl.BlockSpec(memory_space=pltpu.VMEM)


def params(mib):
    return pltpu.CompilerParams(vmem_limit_bytes=mib * MIB)


def attend(queries, keys, values, query_pos):
    rows = queries.shape[0]
    local_heads = queries.shape[1] // HD
    scale = HD ** (-0.5)
    shaped_q = queries.reshape(rows, local_heads, HD)
    latest = jnp.max(query_pos)
    initial = (
        jnp.full((local_heads, rows), -1e30, jnp.float32),
        jnp.zeros((local_heads, rows), jnp.float32),
        jnp.zeros((local_heads, rows, HD), jnp.float32),
    )
    piece_keys = lax.all_gather(keys, "ctx", axis=0, tiled=True)
    piece_values = lax.all_gather(values, "ctx", axis=0, tiled=True)
    count_rows = piece_keys.shape[0]
    span_rows = 2 * rows

    def one_block(block, state):
        offset = block * span_rows
        block_keys = lax.dynamic_slice_in_dim(piece_keys, offset, span_rows, 0).reshape(
            span_rows, local_heads, HD
        )
        block_values = lax.dynamic_slice_in_dim(piece_values, offset, span_rows, 0).reshape(
            span_rows, local_heads, HD
        )
        key_pos = offset + jnp.arange(span_rows, dtype=jnp.int32)

        def compute(inner):
            maxes, totals, accum = inner
            scores = (
                jnp.einsum("qhd,khd->hqk", shaped_q, block_keys, preferred_element_type=jnp.float32)
                * scale
            )
            allowed = key_pos[None, None, :] <= query_pos[None, :, None]
            new_max = jnp.maximum(maxes, jnp.max(jnp.where(allowed, scores, -1e30), axis=-1))
            factor = jnp.exp(maxes - new_max)
            weights = jnp.where(allowed, jnp.exp(scores - new_max[..., None]), 0.0)
            totals = totals * factor + jnp.sum(weights, axis=-1)
            accum = accum * factor[..., None] + jnp.einsum(
                "hqk,khd->hqd",
                weights.astype(jnp.bfloat16),
                block_values,
                preferred_element_type=jnp.float32,
            )
            return (new_max, totals, accum)

        return lax.cond(jnp.min(key_pos) <= latest, compute, lambda inner: inner, state)

    maxes, totals, accum = lax.fori_loop(0, count_rows // span_rows, one_block, initial)
    result = accum / totals[..., None]
    return jnp.transpose(result, (1, 0, 2)).reshape(rows, local_heads * HD).astype(jnp.bfloat16)


def gather_form(attn_query, attn_key, attn_value, out_weight):
    rows = attn_query.shape[0]
    query_pos = lax.axis_index("ctx") * rows + jnp.arange(rows, dtype=jnp.int32)
    heads = attend(attn_query, attn_key, attn_value, query_pos)
    partial_value = jnp.dot(heads, out_weight, preferred_element_type=jnp.float32)
    return lax.psum_scatter(
        partial_value.astype(jnp.bfloat16), "tp", scatter_dimension=1, tiled=True
    )


def pack_kernel(half, me_ref, q_ref, k_ref, v_ref, *refs):
    inner, cross, (held, sem) = refs[:half], refs[half : 2 * half], refs[2 * half :]
    upper, place = me_ref[0] // half, lax.rem(me_ref[0], half)
    copies = [
        pltpu.make_async_copy(ref, held.at[part], sem.at[part])
        for part, ref in enumerate((q_ref, k_ref, v_ref))
    ]
    for one in copies:
        one.start()
    for part, one in enumerate(copies):
        one.wait()
        for shift in range(half):
            goal = place ^ shift
            cols = pl.ds(pl.multiple_of(goal * 2 * HD, 2 * HD), 2 * HD)
            inner[shift][part] = held[part, :, cols]
    for shift in range(half):
        goal = place ^ shift
        even = pl.ds(pl.multiple_of(goal * 2 * HD, HD), HD)
        odd = pl.ds(pl.multiple_of(goal * 2 * HD + HD, HD), HD)

        @pl.when(upper == 0)
        def _():
            cross[shift][0] = held[1, :, odd]
            cross[shift][1] = held[2, :, odd]

        @pl.when(upper == 1)
        def _():
            cross[shift][0] = held[0, :, even]
            cross[shift][1] = held[0, :, even]


def split3(value):
    high = value.astype(jnp.bfloat16)
    value = value - high.astype(jnp.float32)
    middle = value.astype(jnp.bfloat16)
    return high, middle, (value - middle.astype(jnp.float32)).astype(jnp.bfloat16)


def gather(half, place, rows, pieces, part, out, cols=slice(None)):
    for shift in range(half):
        source = place ^ shift
        at = pl.ds(pl.multiple_of(source * rows, rows), rows)
        piece = pieces[shift][part, :, cols]
        out[at, : piece.shape[1]] = piece


def scores(query, keys):
    dims = (((1,), (1,)), ((), ()))
    return lax.dot_general(query, keys, dims, preferred_element_type=jnp.float32)


def weigh(raw, top, values):
    weights = jnp.exp2((raw - top) * (HD ** (-0.5) * LOG2E))
    acc = jnp.dot(weights.astype(jnp.bfloat16), values, preferred_element_type=jnp.float32)
    return acc[:, HD : HD + 1], acc[:, :HD]


def log_sum(top, total):
    return top * (HD ** (-0.5) * LOG2E) + jnp.log2(total)


def inner_kernel(half, me_ref, *refs):
    inner, (even_ref, odd_ref, table_ref) = refs[:half], refs[half:-3]
    q_all, k_all, v_all = refs[-3:]
    rows = inner[0].shape[1]
    place = lax.rem(me_ref[0], half)
    gather(half, place, rows, inner, 0, q_all)
    gather(half, place, rows, inner, 1, k_all)
    for head in range(2):
        one = v_all.at[head]
        gather(half, place, rows, inner, 2, one, slice(head * HD, (head + 1) * HD))
        one[:, HD:] = jnp.ones((half * rows, HD), jnp.bfloat16)
    diag = lax.broadcasted_iota(jnp.int32, (rows, rows), 1) <= lax.broadcasted_iota(
        jnp.int32, (rows, rows), 0
    )
    lane = lax.broadcasted_iota(jnp.int32, (rows, HD), 1)
    table = jnp.zeros((rows, HD), jnp.float32)
    for block in reversed(range(half)):
        lo, hi = block * rows, (block + 1) * rows
        for head in range(2):
            at = slice(head * HD, (head + 1) * HD)
            query = q_all[lo:hi, at]
            last = jnp.where(diag, scores(query, k_all[lo:hi, at]), -1e30)
            top = jnp.max(last, axis=1, keepdims=True)
            if block:
                early = scores(query, k_all[0:lo, at])
                top = jnp.maximum(top, jnp.max(early, axis=1, keepdims=True))
            total, acc = weigh(last, top, v_all[head, lo:hi, :])
            if block:
                total_early, acc_early = weigh(early, top, v_all[head, 0:lo, :])
                total, acc = total + total_early, acc + acc_early
            if head == 0:
                even_ref[lo:hi, :] = (acc / total).astype(jnp.bfloat16)
            else:
                odd_ref[lo:hi, :] = acc / total
            table = jnp.where(lane == head * half + block, log_sum(top, total), table)
    table_ref[...] = table


def cross_kernel(half, me_ref, *refs):
    inner, cross, refs = refs[:half], refs[half : 2 * half], refs[2 * half :]
    (even_ref, odd_ref, table_ref), refs = refs[:3], refs[3:]
    back, over = refs[:half], refs[half : 2 * half]
    q_x, k_x, v_x, o_odd, o_x, stats = refs[2 * half :]
    rows = inner[0].shape[1]
    upper, place = me_ref[0] // half, lax.rem(me_ref[0], half)

    @pl.when(upper == 0)
    def _():
        gather(half, place, rows, cross, 0, q_x)
        gather(half, place, rows, inner, 1, k_x, slice(0, HD))
        gather(half, place, rows, inner, 2, v_x, slice(0, HD))

    @pl.when(upper == 1)
    def _():
        gather(half, place, rows, inner, 0, q_x, slice(HD, 2 * HD))
        gather(half, place, rows, cross, 0, k_x)
        gather(half, place, rows, cross, 1, v_x)

    v_x[:, HD:] = jnp.ones((half * rows, HD), jnp.bfloat16)
    lane = lax.broadcasted_iota(jnp.int32, (rows, HD), 1)
    logs = table_ref[...]
    table = logs
    for block in range(half):
        lo, hi = block * rows, (block + 1) * rows
        raw = scores(q_x[lo:hi, :], k_x[...])
        top = jnp.max(raw, axis=1, keepdims=True)
        total, acc = weigh(raw, top, v_x[...])
        result = acc / total
        o_x[lo:hi, :] = result.astype(jnp.bfloat16)
        log_x = log_sum(top, total)
        table = jnp.where(lane == half + block, log_x, table)
        gap = jnp.where(upper == 1, log_x - logs[:, half + block : half + block + 1], -1e30)
        near, far = 1.0 / (1.0 + jnp.exp2(gap)), 1.0 / (1.0 + jnp.exp2(-gap))
        o_odd[lo:hi, :] = (near * odd_ref[lo:hi, :] + far * result).astype(jnp.bfloat16)
    turned = jnp.transpose(table)
    for i, part in enumerate(split3(turned[0 : 2 * half, :])):
        stats[i] = part.astype(jnp.float32)
    for shift in range(half):
        goal = place ^ shift
        at = pl.ds(pl.multiple_of(goal * rows, rows), rows)
        back[shift][0:rows, :HD] = even_ref[at, :]
        back[shift][0:rows, HD:] = o_odd[at, :]
        over[shift][0:rows, :] = o_x[at, :]
        for out, first in ((back[shift], 0), (over[shift], half)):
            wide = out.shape[1]
            lines = [stats[i, pl.ds(first + goal, 1), :] for i in range(3)]
            lines = [line[:, at : at + wide] for line in lines for at in range(0, rows, wide)]
            empty = jnp.zeros((STAT_ROWS - len(lines), wide), jnp.float32)
            out[rows:, :] = jnp.concatenate(lines + [empty], axis=0).astype(jnp.bfloat16)


def assemble(half, me_ref, back, over, heads):
    rows = heads.shape[0]
    upper, place = me_ref[0] // half, lax.rem(me_ref[0], half)

    def read_log(piece):
        steps = rows // piece.shape[1]
        block = piece[rows:, :].astype(jnp.float32)
        sums = [
            block[i : i + 1, :] + block[steps + i : steps + i + 1, :]
            + block[2 * steps + i : 2 * steps + i + 1, :]
            for i in range(steps)
        ]
        return jnp.concatenate(sums, axis=1)

    gaps = []
    for shift in range(half):
        gap = read_log(over[shift]) - read_log(back[shift])
        gaps.append(jnp.where(upper == 1, gap, -1e30))
    table = jnp.concatenate(gaps + [jnp.zeros((HD - half, rows), jnp.float32)], axis=0)
    table = jnp.transpose(table)
    for shift in range(half):
        source = place ^ shift
        even = pl.ds(pl.multiple_of(source * 2 * HD, HD), HD)
        odd = pl.ds(pl.multiple_of(source * 2 * HD + HD, HD), HD)
        gap = table[:, shift : shift + 1]
        near = 1.0 / (1.0 + jnp.exp2(gap))
        far = 1.0 / (1.0 + jnp.exp2(-gap))
        merged = near * back[shift][0:rows, 0:HD].astype(jnp.float32)
        merged += far * over[shift][0:rows, :].astype(jnp.float32)
        heads[:, even] = merged.astype(jnp.bfloat16)
        heads[:, odd] = back[shift][0:rows, HD:]


def multiply(heads, weight, out, tile, start=0):
    for at in range(0, out.shape[1], tile):
        out[:, at : at + tile] = jnp.dot(
            heads[...],
            weight[:, start + at : start + at + tile],
            preferred_element_type=jnp.float32,
        ).astype(jnp.bfloat16)


def first_kernel(half, tile, me_ref, *refs):
    back, over, (weight, heads, out) = refs[:half], refs[half : 2 * half], refs[2 * half :]
    assemble(half, me_ref, back, over, heads)
    multiply(heads, weight, out, tile)


def later_kernel(tile, start, heads, *refs):
    count = len(refs) // 2
    for weight, out in zip(refs[:count], refs[count:]):
        multiply(heads, weight, out, tile, start)


def last_kernel(keep, *refs):
    swapped, (whole, out, held, sem) = refs[:OWN_PARTS], refs[OWN_PARTS:]
    rows, cols = keep.shape
    step, wide = rows // STEPS, cols // OWN_PARTS
    copies = []
    for i in range(STEPS):
        at = slice(i * step, (i + 1) * step)
        for j, part in enumerate(swapped):
            here = slice(j * wide, (j + 1) * wide)
            total = keep[at, here].astype(jnp.float32) + part[at, :].astype(jnp.float32)
            held[at, here] = (total + whole[at, here].astype(jnp.float32)).astype(jnp.bfloat16)
        rows_at = pl.ds(i * step, step)
        copies.append(pltpu.make_async_copy(held.at[rows_at], out.at[rows_at], sem.at[i]))
        copies[-1].start()
    for one in copies:
        one.wait()


def project(heads, weights, start, cols):
    out = jax.ShapeDtypeStruct((heads.shape[0], cols), jnp.bfloat16)
    return pl.pallas_call(
        functools.partial(later_kernel, 512, start),
        in_specs=[VMEM] * (1 + len(weights)),
        out_specs=[VMEM] * len(weights),
        out_shape=[out] * len(weights),
        compiler_params=params(16),
        cost_estimate=COST,
    )(heads, *weights)


def fetch_kernel(place_ref, w_ref, *refs):
    outs, sem = refs[:-1], refs[-1]
    cols = outs[0].shape[1]
    copies = []
    for which, out in enumerate(outs):
        at = pl.ds(pl.multiple_of(place_ref[1 + which], cols), cols)
        copies.append(pltpu.make_async_copy(w_ref.at[:, at], out, sem.at[which]))
    for one in copies:
        one.start()
    for one in copies:
        one.wait()


def fetch(place, weight, cols):
    depth, groups = weight.shape[0], place.shape[0] - 1
    return pl.pallas_call(
        fetch_kernel,
        in_specs=[pl.BlockSpec(memory_space=pltpu.SMEM), pl.BlockSpec(memory_space=pl.ANY)],
        out_specs=[VMEM] * groups,
        out_shape=[jax.ShapeDtypeStruct((depth, cols), weight.dtype)] * groups,
        scratch_shapes=[pltpu.SemaphoreType.DMA((groups,))],
        compiler_params=params(FETCH_MIB),
        cost_estimate=pl.CostEstimate(
            flops=1, bytes_accessed=4 * depth * cols * groups, transcendentals=1
        ),
    )(place, weight)


def heads_form(attn_query, attn_key, attn_value, out_weight):
    n, tp = lax.axis_size("ctx"), lax.axis_size("tp")
    half = n // 2
    rows = attn_query.shape[0]
    bf16, f32 = jnp.bfloat16, jnp.float32
    me, mine = lax.axis_index("ctx"), lax.axis_index("tp")
    place = me.astype(jnp.int32).reshape(1)
    smem = pl.BlockSpec(memory_space=pltpu.SMEM)

    def within(shift):
        return [(i, i ^ shift) for i in range(n)]

    def between(shift, lower, upper):
        up = [(i, half + (i ^ shift)) for i in range(half)]
        down = [(half + i, i ^ shift) for i in range(half)]
        return up * lower + down * upper

    inner_shape = jax.ShapeDtypeStruct((3, rows, 2 * HD), bf16)
    cross_shape = jax.ShapeDtypeStruct((2, rows, HD), bf16)
    packed = pl.pallas_call(
        functools.partial(pack_kernel, half),
        in_specs=[smem] + [pl.BlockSpec(memory_space=pl.ANY)] * 3,
        out_specs=[VMEM] * n,
        out_shape=[inner_shape] * half + [cross_shape] * half,
        scratch_shapes=[
            pltpu.VMEM((3, rows, n * HD), bf16),
            pltpu.SemaphoreType.DMA((3,)),
        ],
        compiler_params=params(56),
        cost_estimate=COST,
    )(place, attn_query, attn_key, attn_value)
    inner, cross = list(packed[:half]), list(packed[half:])

    cols = out_weight.shape[1] // tp
    planes = tp // 2
    y, core = mine // 2, lax.rem(mine, 2)
    swap = [(i, i ^ 1) for i in range(tp)]

    def wanted(plane):
        groups = [2 * plane + 1 - core, 2 * plane + core]
        return jnp.stack([me] + [group * cols for group in groups]).astype(jnp.int32)

    near = [
        fetch(wanted(lax.rem(y + shift, planes)), out_weight, cols) for shift in range(1, planes)
    ]
    for shift in range(1, half):
        inner[shift] = lax.ppermute(inner[shift], "ctx", within(shift))
    cross = [
        lax.ppermute(piece, "ctx", between(shift, 1, 1)) for shift, piece in enumerate(cross)
    ]

    inner[1], *rest = lax.optimization_barrier((inner[1], *inner[2:], near))
    inner[2:], near = rest[:-1], rest[-1]
    back_shape = jax.ShapeDtypeStruct((rows + STAT_ROWS, 2 * HD), bf16)
    over_shape = jax.ShapeDtypeStruct((rows + STAT_ROWS, HD), bf16)
    big, small = pltpu.VMEM((half * rows, 2 * HD), bf16), pltpu.VMEM((half * rows, HD), bf16)
    results = pl.pallas_call(
        functools.partial(inner_kernel, half),
        in_specs=[smem] + [VMEM] * half,
        out_specs=[VMEM] * 3,
        out_shape=[
            jax.ShapeDtypeStruct((half * rows, HD), bf16),
            jax.ShapeDtypeStruct((half * rows, HD), f32),
            jax.ShapeDtypeStruct((rows, HD), f32),
        ],
        scratch_shapes=[big] * 2 + [pltpu.VMEM((2, half * rows, 2 * HD), bf16)],
        compiler_params=params(24),
        cost_estimate=COST,
    )(place, *inner)
    outs = pl.pallas_call(
        functools.partial(cross_kernel, half),
        in_specs=[smem] + [VMEM] * (n + 3),
        out_specs=[VMEM] * n,
        out_shape=[back_shape] * half + [over_shape] * half,
        scratch_shapes=[small] * 2 + [big] + [small] * 2 + [ pltpu.VMEM((3, n, rows), f32)],
        compiler_params=params(24),
        cost_estimate=COST,
    )(place, *inner, *cross, *results)
    back, over = list(outs[:half]), list(outs[half:])
    for shift in range(1, half):
        back[shift] = lax.ppermute(back[shift], "ctx", within(shift))
    for shift in range(half):
        if shift in T2TIE:
            over[shift], back[1] = lax.optimization_barrier((over[shift], back[1]))
        over[shift] = lax.ppermute(over[shift], "ctx", between(shift, 1, 0))

    tied = (back[1], *over, *back[2:])
    back[1], *tied = lax.optimization_barrier(tied)
    over, back[2:] = tied[:half], tied[half:]
    heads, crossing = None, []
    for shift, (w_give, w_keep) in enumerate(near, 1):
        perm = [(i, (i + 2 * shift) % tp) for i in range(tp)]
        if heads is None:
            heads, give = pl.pallas_call(
                functools.partial(first_kernel, half, 512),
                in_specs=[smem] + [VMEM] * (n + 1),
                out_specs=[VMEM] * 2,
                out_shape=[
                    jax.ShapeDtypeStruct((rows, n * HD), bf16),
                    jax.ShapeDtypeStruct((rows, cols // 2), bf16),
                ],
                compiler_params=params(16),
                cost_estimate=COST,
            )(place, *back, *over, w_give)
        else:
            (give,) = project(heads, [w_give], 0, cols // 2)
        (rest,) = project(heads, [w_give], cols // 2, cols // 2)
        (keep,) = project(heads, [w_keep], 0, cols)
        came = [lax.ppermute(one, "tp", swap).astype(f32) for one in (give, rest)]
        both = (keep.astype(f32) + jnp.concatenate(came, axis=1)).astype(bf16)
        crossing.append(lax.ppermute(both, "tp", perm))
        both, heads = lax.optimization_barrier((both, heads))
    out_weight, heads = lax.optimization_barrier((out_weight, heads))
    give, keep = project(heads, fetch(wanted(y), out_weight, cols), 0, cols)
    piece = cols // OWN_PARTS
    swapped = [
        lax.ppermute(give[:, at : at + piece], "tp", swap) for at in range(0, cols, piece)
    ]
    whole = crossing[0]
    if len(crossing) > 1:
        whole = sum(one.astype(f32) for one in crossing)
    return pl.pallas_call(
        last_kernel,
        in_specs=[VMEM] * (2 + OWN_PARTS),
        out_specs=pl.BlockSpec(memory_space=pl.ANY),
        out_shape=jax.ShapeDtypeStruct((rows, cols), bf16),
        scratch_shapes=[
            pltpu.VMEM((rows, cols), bf16),
            pltpu.SemaphoreType.DMA((STEPS,)),
        ],
        compiler_params=params(16),
        cost_estimate=COST,
    )(keep, *swapped, whole)


def solution(mesh):
    def per_device(attn_query, attn_key, attn_value, out_weight):
        heads, n, tp = attn_query.shape[1] // HD, mesh.shape["ctx"], mesh.shape["tp"]
        paired = heads == n and n > 2 and n & (n - 1) == 0 and n <= HD and tp % 2 == 0 and tp > 2
        form = heads_form if paired and attn_query.shape[0] == 2 * HD else gather_form
        return form(attn_query, attn_key, attn_value, out_weight)

    return jax.shard_map(
        per_device,
        mesh=mesh,
        in_specs=(P("ctx", "tp"), P("ctx", "tp"), P("ctx", "tp"), P("tp", None)),
        out_specs=P("ctx", "tp"),
        check_vma=False,
    )
```

```python
import functools

import jax
import jax.numpy as jnp
from jax import lax
from jax.experimental import pallas as pl
from jax.experimental.pallas import tpu as pltpu
from jax.sharding import PartitionSpec as P

HD = 128
MIB = 1 << 20
OWN_PARTS = 2
STEPS = 4
STAT_ROWS = 16
T2TIE = (2, 3)
LOG2E = 1.4426950408889634
FETCH_MIB = 40
COST = pl.CostEstimate(flops=1, bytes_accessed=1, transcendentals=1)
VMEM = pl.BlockSpec(memory_space=pltpu.VMEM)


def params(mib):
    return pltpu.CompilerParams(vmem_limit_bytes=mib * MIB)


def attend(queries, keys, values, query_pos):
    rows = queries.shape[0]
    local_heads = queries.shape[1] // HD
    scale = HD ** (-0.5)
    shaped_q = queries.reshape(rows, local_heads, HD)
    latest = jnp.max(query_pos)
    initial = (
        jnp.full((local_heads, rows), -1e30, jnp.float32),
        jnp.zeros((local_heads, rows), jnp.float32),
        jnp.zeros((local_heads, rows, HD), jnp.float32),
    )
    piece_keys = lax.all_gather(keys, "ctx", axis=0, tiled=True)
    piece_values = lax.all_gather(values, "ctx", axis=0, tiled=True)
    count_rows = piece_keys.shape[0]
    span_rows = 2 * rows

    def one_block(block, state):
        offset = block * span_rows
        block_keys = lax.dynamic_slice_in_dim(piece_keys, offset, span_rows, 0).reshape(
            span_rows, local_heads, HD
        )
        block_values = lax.dynamic_slice_in_dim(piece_values, offset, span_rows, 0).reshape(
            span_rows, local_heads, HD
        )
        key_pos = offset + jnp.arange(span_rows, dtype=jnp.int32)

        def compute(inner):
            maxes, totals, accum = inner
            scores = (
                jnp.einsum("qhd,khd->hqk", shaped_q, block_keys, preferred_element_type=jnp.float32)
                * scale
            )
            allowed = key_pos[None, None, :] <= query_pos[None, :, None]
            new_max = jnp.maximum(maxes, jnp.max(jnp.where(allowed, scores, -1e30), axis=-1))
            factor = jnp.exp(maxes - new_max)
            weights = jnp.where(allowed, jnp.exp(scores - new_max[..., None]), 0.0)
            totals = totals * factor + jnp.sum(weights, axis=-1)
            accum = accum * factor[..., None] + jnp.einsum(
                "hqk,khd->hqd",
                weights.astype(jnp.bfloat16),
                block_values,
                preferred_element_type=jnp.float32,
            )
            return (new_max, totals, accum)

        return lax.cond(jnp.min(key_pos) <= latest, compute, lambda inner: inner, state)

    maxes, totals, accum = lax.fori_loop(0, count_rows // span_rows, one_block, initial)
    result = accum / totals[..., None]
    return jnp.transpose(result, (1, 0, 2)).reshape(rows, local_heads * HD).astype(jnp.bfloat16)


def gather_form(attn_query, attn_key, attn_value, out_weight):
    rows = attn_query.shape[0]
    query_pos = lax.axis_index("ctx") * rows + jnp.arange(rows, dtype=jnp.int32)
    heads = attend(attn_query, attn_key, attn_value, query_pos)
    partial_value = jnp.dot(heads, out_weight, preferred_element_type=jnp.float32)
    return lax.psum_scatter(
        partial_value.astype(jnp.bfloat16), "tp", scatter_dimension=1, tiled=True
    )


def pack_kernel(half, me_ref, q_ref, k_ref, v_ref, *refs):
    inner, cross, (held, sem) = refs[:half], refs[half : 2 * half], refs[2 * half :]
    upper, place = me_ref[0] // half, lax.rem(me_ref[0], half)
    copies = [
        pltpu.make_async_copy(ref, held.at[part], sem.at[part])
        for part, ref in enumerate((q_ref, k_ref, v_ref))
    ]
    for one in copies:
        one.start()
    for part, one in enumerate(copies):
        one.wait()
        for shift in range(half):
            goal = place ^ shift
            cols = pl.ds(pl.multiple_of(goal * 2 * HD, 2 * HD), 2 * HD)
            inner[shift][part] = held[part, :, cols]
    for shift in range(half):
        goal = place ^ shift
        even = pl.ds(pl.multiple_of(goal * 2 * HD, HD), HD)
        odd = pl.ds(pl.multiple_of(goal * 2 * HD + HD, HD), HD)

        @pl.when(upper == 0)
        def _():
            cross[shift][0] = held[1, :, odd]
            cross[shift][1] = held[2, :, odd]

        @pl.when(upper == 1)
        def _():
            cross[shift][0] = held[0, :, even]
            cross[shift][1] = held[0, :, even]


def split3(value):
    high = value.astype(jnp.bfloat16)
    value = value - high.astype(jnp.float32)
    middle = value.astype(jnp.bfloat16)
    return high, middle, (value - middle.astype(jnp.float32)).astype(jnp.bfloat16)


def gather(half, place, rows, pieces, part, out, cols=slice(None)):
    for shift in range(half):
        source = place ^ shift
        at = pl.ds(pl.multiple_of(source * rows, rows), rows)
        piece = pieces[shift][part, :, cols]
        out[at, : piece.shape[1]] = piece


def scores(query, keys):
    dims = (((1,), (1,)), ((), ()))
    return lax.dot_general(query, keys, dims, preferred_element_type=jnp.float32)


def weigh(raw, top, values):
    weights = jnp.exp2((raw - top) * (HD ** (-0.5) * LOG2E))
    acc = jnp.dot(weights.astype(jnp.bfloat16), values, preferred_element_type=jnp.float32)
    return acc[:, HD : HD + 1], acc[:, :HD]


def log_sum(top, total):
    return top * (HD ** (-0.5) * LOG2E) + jnp.log2(total)


def inner_kernel(half, me_ref, *refs):
    inner, (even_ref, odd_ref, table_ref) = refs[:half], refs[half:-3]
    q_all, k_all, v_all = refs[-3:]
    rows = inner[0].shape[1]
    place = lax.rem(me_ref[0], half)
    gather(half, place, rows, inner, 0, q_all)
    gather(half, place, rows, inner, 1, k_all)
    for head in range(2):
        one = v_all.at[head]
        gather(half, place, rows, inner, 2, one, slice(head * HD, (head + 1) * HD))
        one[:, HD:] = jnp.ones((half * rows, HD), jnp.bfloat16)
    diag = lax.broadcasted_iota(jnp.int32, (rows, rows), 1) <= lax.broadcasted_iota(
        jnp.int32, (rows, rows), 0
    )
    lane = lax.broadcasted_iota(jnp.int32, (rows, HD), 1)
    table = jnp.zeros((rows, HD), jnp.float32)
    for block in reversed(range(half)):
        lo, hi = block * rows, (block + 1) * rows
        for head in range(2):
            at = slice(head * HD, (head + 1) * HD)
            query = q_all[lo:hi, at]
            last = jnp.where(diag, scores(query, k_all[lo:hi, at]), -1e30)
            top = jnp.max(last, axis=1, keepdims=True)
            if block:
                early = scores(query, k_all[0:lo, at])
                top = jnp.maximum(top, jnp.max(early, axis=1, keepdims=True))
            total, acc = weigh(last, top, v_all[head, lo:hi, :])
            if block:
                total_early, acc_early = weigh(early, top, v_all[head, 0:lo, :])
                total, acc = total + total_early, acc + acc_early
            if head == 0:
                even_ref[lo:hi, :] = (acc / total).astype(jnp.bfloat16)
            else:
                odd_ref[lo:hi, :] = acc / total
            table = jnp.where(lane == head * half + block, log_sum(top, total), table)
    table_ref[...] = table


def cross_kernel(half, me_ref, *refs):
    inner, cross, refs = refs[:half], refs[half : 2 * half], refs[2 * half :]
    (even_ref, odd_ref, table_ref), refs = refs[:3], refs[3:]
    back, over = refs[:half], refs[half : 2 * half]
    q_x, k_x, v_x, o_odd, o_x, stats = refs[2 * half :]
    rows = inner[0].shape[1]
    upper, place = me_ref[0] // half, lax.rem(me_ref[0], half)

    @pl.when(upper == 0)
    def _():
        gather(half, place, rows, cross, 0, q_x)
        gather(half, place, rows, inner, 1, k_x, slice(0, HD))
        gather(half, place, rows, inner, 2, v_x, slice(0, HD))

    @pl.when(upper == 1)
    def _():
        gather(half, place, rows, inner, 0, q_x, slice(HD, 2 * HD))
        gather(half, place, rows, cross, 0, k_x)
        gather(half, place, rows, cross, 1, v_x)

    v_x[:, HD:] = jnp.ones((half * rows, HD), jnp.bfloat16)
    lane = lax.broadcasted_iota(jnp.int32, (rows, HD), 1)
    logs = table_ref[...]
    table = logs
    for block in range(half):
        lo, hi = block * rows, (block + 1) * rows
        raw = scores(q_x[lo:hi, :], k_x[...])
        top = jnp.max(raw, axis=1, keepdims=True)
        total, acc = weigh(raw, top, v_x[...])
        result = acc / total
        o_x[lo:hi, :] = result.astype(jnp.bfloat16)
        log_x = log_sum(top, total)
        table = jnp.where(lane == half + block, log_x, table)
        gap = jnp.where(upper == 1, log_x - logs[:, half + block : half + block + 1], -1e30)
        near, far = 1.0 / (1.0 + jnp.exp2(gap)), 1.0 / (1.0 + jnp.exp2(-gap))
        o_odd[lo:hi, :] = (near * odd_ref[lo:hi, :] + far * result).astype(jnp.bfloat16)
    turned = jnp.transpose(table)
    for i, part in enumerate(split3(turned[0 : 2 * half, :])):
        stats[i] = part.astype(jnp.float32)
    for shift in range(half):
        goal = place ^ shift
        at = pl.ds(pl.multiple_of(goal * rows, rows), rows)
        back[shift][0:rows, :HD] = even_ref[at, :]
        back[shift][0:rows, HD:] = o_odd[at, :]
        over[shift][0:rows, :] = o_x[at, :]
        for out, first in ((back[shift], 0), (over[shift], half)):
            wide = out.shape[1]
            lines = [stats[i, pl.ds(first + goal, 1), :] for i in range(3)]
            lines = [line[:, at : at + wide] for line in lines for at in range(0, rows, wide)]
            empty = jnp.zeros((STAT_ROWS - len(lines), wide), jnp.float32)
            out[rows:, :] = jnp.concatenate(lines + [empty], axis=0).astype(jnp.bfloat16)


def assemble(half, me_ref, back, over, heads):
    rows = heads.shape[0]
    upper, place = me_ref[0] // half, lax.rem(me_ref[0], half)

    def read_log(piece):
        steps = rows // piece.shape[1]
        block = piece[rows:, :].astype(jnp.float32)
        sums = [
            block[i : i + 1, :] + block[steps + i : steps + i + 1, :]
            + block[2 * steps + i : 2 * steps + i + 1, :]
            for i in range(steps)
        ]
        return jnp.concatenate(sums, axis=1)

    gaps = []
    for shift in range(half):
        gap = read_log(over[shift]) - read_log(back[shift])
        gaps.append(jnp.where(upper == 1, gap, -1e30))
    table = jnp.concatenate(gaps + [jnp.zeros((HD - half, rows), jnp.float32)], axis=0)
    table = jnp.transpose(table)
    for shift in range(half):
        source = place ^ shift
        even = pl.ds(pl.multiple_of(source * 2 * HD, HD), HD)
        odd = pl.ds(pl.multiple_of(source * 2 * HD + HD, HD), HD)
        gap = table[:, shift : shift + 1]
        near = 1.0 / (1.0 + jnp.exp2(gap))
        far = 1.0 / (1.0 + jnp.exp2(-gap))
        merged = near * back[shift][0:rows, 0:HD].astype(jnp.float32)
        merged += far * over[shift][0:rows, :].astype(jnp.float32)
        heads[:, even] = merged.astype(jnp.bfloat16)
        heads[:, odd] = back[shift][0:rows, HD:]


def multiply(heads, weight, out, tile):
    for at in range(0, out.shape[1], tile):
        out[:, at : at + tile] = jnp.dot(
            heads[...], weight[:, at : at + tile], preferred_element_type=jnp.float32
        ).astype(jnp.bfloat16)


def first_kernel(half, tile, me_ref, *refs):
    over, back, (weight, heads, out) = refs[:half], refs[half : 2 * half], refs[2 * half :]
    assemble(half, me_ref, back, over, heads)
    multiply(heads, weight, out, tile)


def later_kernel(tile, heads, *refs):
    count = len(refs) // 2
    for weight, out in zip(refs[:count], refs[count:]):
        multiply(heads, weight, out, tile)


def last_kernel(keep, *refs):
    swapped, (whole, out, held, sem) = refs[:OWN_PARTS], refs[OWN_PARTS:]
    rows, cols = keep.shape
    step, wide = rows // STEPS, cols // OWN_PARTS
    copies = []
    for i in range(STEPS):
        at = slice(i * step, (i + 1) * step)
        for j, part in enumerate(swapped):
            here = slice(j * wide, (j + 1) * wide)
            total = keep[at, here].astype(jnp.float32) + part[at, :].astype(jnp.float32)
            held[at, here] = (total + whole[at, here].astype(jnp.float32)).astype(jnp.bfloat16)
        rows_at = pl.ds(i * step, step)
        copies.append(pltpu.make_async_copy(held.at[rows_at], out.at[rows_at], sem.at[i]))
        copies[-1].start()
    for one in copies:
        one.wait()


def project(heads, weights):
    out = jax.ShapeDtypeStruct((heads.shape[0], weights[0].shape[1]), jnp.bfloat16)
    return pl.pallas_call(
        functools.partial(later_kernel, 512),
        in_specs=[VMEM] * (1 + len(weights)),
        out_specs=[VMEM] * len(weights),
        out_shape=[out] * len(weights),
        compiler_params=params(16),
        cost_estimate=COST,
    )(heads, *weights)


def fetch_kernel(place_ref, w_ref, *refs):
    outs, sem = refs[:-1], refs[-1]
    cols = outs[0].shape[1]
    copies = []
    for which, out in enumerate(outs):
        at = pl.ds(pl.multiple_of(place_ref[1 + which], cols), cols)
        copies.append(pltpu.make_async_copy(w_ref.at[:, at], out, sem.at[which]))
    for one in copies:
        one.start()
    for one in copies:
        one.wait()


def fetch(place, weight, cols):
    depth, groups = weight.shape[0], place.shape[0] - 1
    return pl.pallas_call(
        fetch_kernel,
        in_specs=[pl.BlockSpec(memory_space=pltpu.SMEM), pl.BlockSpec(memory_space=pl.ANY)],
        out_specs=[VMEM] * groups,
        out_shape=[jax.ShapeDtypeStruct((depth, cols), weight.dtype)] * groups,
        scratch_shapes=[pltpu.SemaphoreType.DMA((groups,))],
        compiler_params=params(FETCH_MIB),
        cost_estimate=pl.CostEstimate(
            flops=1, bytes_accessed=4 * depth * cols * groups, transcendentals=1
        ),
    )(place, weight)


def heads_form(attn_query, attn_key, attn_value, out_weight):
    n, tp = lax.axis_size("ctx"), lax.axis_size("tp")
    half = n // 2
    rows = attn_query.shape[0]
    bf16, f32 = jnp.bfloat16, jnp.float32
    me, mine = lax.axis_index("ctx"), lax.axis_index("tp")
    place = me.astype(jnp.int32).reshape(1)
    smem = pl.BlockSpec(memory_space=pltpu.SMEM)

    def within(shift):
        return [(i, i ^ shift) for i in range(n)]

    def between(shift, lower, upper):
        up = [(i, half + (i ^ shift)) for i in range(half)]
        down = [(half + i, i ^ shift) for i in range(half)]
        return up * lower + down * upper

    inner_shape = jax.ShapeDtypeStruct((3, rows, 2 * HD), bf16)
    cross_shape = jax.ShapeDtypeStruct((2, rows, HD), bf16)
    packed = pl.pallas_call(
        functools.partial(pack_kernel, half),
        in_specs=[smem] + [pl.BlockSpec(memory_space=pl.ANY)] * 3,
        out_specs=[VMEM] * n,
        out_shape=[inner_shape] * half + [cross_shape] * half,
        scratch_shapes=[
            pltpu.VMEM((3, rows, n * HD), bf16),
            pltpu.SemaphoreType.DMA((3,)),
        ],
        compiler_params=params(56),
        cost_estimate=COST,
    )(place, attn_query, attn_key, attn_value)
    inner, cross = list(packed[:half]), list(packed[half:])

    cols = out_weight.shape[1] // tp
    planes = tp // 2
    y, core = mine // 2, lax.rem(mine, 2)
    swap = [(i, i ^ 1) for i in range(tp)]

    def wanted(plane):
        groups = [2 * plane + 1 - core, 2 * plane + core]
        return jnp.stack([me] + [group * cols for group in groups]).astype(jnp.int32)

    near = [
        fetch(wanted(lax.rem(y + shift, planes)), out_weight, cols) for shift in range(1, planes)
    ]
    for shift in range(1, half):
        inner[shift] = lax.ppermute(inner[shift], "ctx", within(shift))
    cross = [
        lax.ppermute(piece, "ctx", between(shift, 1, 1)) for shift, piece in enumerate(cross)
    ]

    inner[1], *rest = lax.optimization_barrier((inner[1], *inner[2:], near))
    inner[2:], near = rest[:-1], rest[-1]
    back_shape = jax.ShapeDtypeStruct((rows + STAT_ROWS, 2 * HD), bf16)
    over_shape = jax.ShapeDtypeStruct((rows + STAT_ROWS, HD), bf16)
    big, small = pltpu.VMEM((half * rows, 2 * HD), bf16), pltpu.VMEM((half * rows, HD), bf16)
    results = pl.pallas_call(
        functools.partial(inner_kernel, half),
        in_specs=[smem] + [VMEM] * half,
        out_specs=[VMEM] * 3,
        out_shape=[
            jax.ShapeDtypeStruct((half * rows, HD), bf16),
            jax.ShapeDtypeStruct((half * rows, HD), f32),
            jax.ShapeDtypeStruct((rows, HD), f32),
        ],
        scratch_shapes=[big] * 2 + [pltpu.VMEM((2, half * rows, 2 * HD), bf16)],
        compiler_params=params(24),
        cost_estimate=COST,
    )(place, *inner)
    outs = pl.pallas_call(
        functools.partial(cross_kernel, half),
        in_specs=[smem] + [VMEM] * (n + 3),
        out_specs=[VMEM] * n,
        out_shape=[back_shape] * half + [over_shape] * half,
        scratch_shapes=[small] * 2 + [big] + [small] * 2 + [ pltpu.VMEM((3, n, rows), f32)],
        compiler_params=params(24),
        cost_estimate=COST,
    )(place, *inner, *cross, *results)
    back, over = list(outs[:half]), list(outs[half:])
    for shift in range(1, half):
        back[shift] = lax.ppermute(back[shift], "ctx", within(shift))
    for shift in range(half):
        if shift in T2TIE:
            over[shift], back[1] = lax.optimization_barrier((over[shift], back[1]))
        over[shift] = lax.ppermute(over[shift], "ctx", between(shift, 1, 0))

    heads, crossing = None, []
    for shift, (w_give, w_keep) in enumerate(near, 1):
        perm = [(i, (i + 2 * shift) % tp) for i in range(tp)]
        if heads is None:
            heads, give = pl.pallas_call(
                functools.partial(first_kernel, half, 512),
                in_specs=[smem] + [VMEM] * (n + 1),
                out_specs=[VMEM] * 2,
                out_shape=[
                    jax.ShapeDtypeStruct((rows, n * HD), bf16),
                    jax.ShapeDtypeStruct((rows, cols), bf16),
                ],
                compiler_params=params(16),
                cost_estimate=COST,
            )(place, *over, *back, w_give)
        else:
            (give,) = project(heads, [w_give])
        (keep,) = project(heads, [w_keep])
        both = (keep.astype(f32) + lax.ppermute(give, "tp", swap).astype(f32)).astype(bf16)
        crossing.append(lax.ppermute(both, "tp", perm))
        both, heads = lax.optimization_barrier((both, heads))
    out_weight, heads = lax.optimization_barrier((out_weight, heads))
    give, keep = project(heads, fetch(wanted(y), out_weight, cols))
    piece = cols // OWN_PARTS
    swapped = [
        lax.ppermute(give[:, at : at + piece], "tp", swap) for at in range(0, cols, piece)
    ]
    whole = crossing[0]
    if len(crossing) > 1:
        whole = sum(one.astype(f32) for one in crossing)
    return pl.pallas_call(
        last_kernel,
        in_specs=[VMEM] * (2 + OWN_PARTS),
        out_specs=pl.BlockSpec(memory_space=pl.ANY),
        out_shape=jax.ShapeDtypeStruct((rows, cols), bf16),
        scratch_shapes=[
            pltpu.VMEM((rows, cols), bf16),
            pltpu.SemaphoreType.DMA((STEPS,)),
        ],
        compiler_params=params(16),
        cost_estimate=COST,
    )(keep, *swapped, whole)


def solution(mesh):
    def per_device(attn_query, attn_key, attn_value, out_weight):
        heads, n, tp = attn_query.shape[1] // HD, mesh.shape["ctx"], mesh.shape["tp"]
        paired = heads == n and n > 2 and n & (n - 1) == 0 and n <= HD and tp % 2 == 0 and tp > 2
        form = heads_form if paired and attn_query.shape[0] == 2 * HD else gather_form
        return form(attn_query, attn_key, attn_value, out_weight)

    return jax.shard_map(
        per_device,
        mesh=mesh,
        in_specs=(P("ctx", "tp"), P("ctx", "tp"), P("ctx", "tp"), P("tp", None)),
        out_specs=P("ctx", "tp"),
        check_vma=False,
    )
```
